512 devices in a mesh: cfd: 64 (over y, z), obs: 8 (over x, core).
Axes of the slice: x: 4, y: 4, z: 16, core: 2. Of those that a mesh axis runs over, the one named last changes fastest.
Arguments:
- flow_field: float32 [4, 1024, 128, 128], P(None, 'cfd', 'obs'), may hold values from -6 to 6
- disk_mask: int32 [1024, 128, 128], P('cfd', 'obs'), may hold values 0 or 1
- surf_cell: int32 [8, 8192], P('obs', 'cfd'), may hold values from 0 to 32767
- delay_bin: int32 [8, 8192], P('obs', 'cfd'), may hold values from 0 to 505
- tap_phase: int32 [8, 8192], P('obs', 'cfd'), may hold values from 0 to 3
- panel_counts: int32 [8, 64], replicated, may hold values from 1 to 128, 4096 in all within a row
- observer_pos: float32 [3, 8192], P(None, 'cfd'), may hold values from 0 to 1
Outputs:
- flow_out: float32 [4, 1024, 128, 128], P(None, 'cfd', 'obs')
- pressure_signal: float32 [8192, 512], P(('cfd', 'obs'))
The draws below stay inside these ranges and needn't reach their ends.
Inputs may be any that keep to these rules, and one draw needn't show every extreme that they name: `panel_counts`: every row sums to 4096, and every row has an entry equal to 128.
All inputs are finite; a program needn't handle non-finite values. No bound on the sum of `disk_mask` on one device may be relied on, other than what follows from the above.
Results may differ from the reference program's by a relative error of at most 0.0041.
Values sent between devices are 32-bit elements; how exact they have to be, the bound alone decides.
A program may use at most 128 MiB of HBM per device.

```python
import math
import jax
import jax.numpy as jnp
import numpy as np
from jax import lax

CX = 16
CY = 16
CZ = 128
STEPS = 4
SAMPLES = 512
PMAX = 128
GX = 1024
GY = 128
GZ = 128
PAN_COL = 4096
OBSERVERS = 8192
N_CFD = 64
N_OBS = 8


def place_ends(result, rng, low, largest):
    shape = result.shape
    spot = [jax.random.randint(jax.random.fold_in(rng, axis), (), 0, shape[axis]) for axis in range(len(shape))]
    result = result.at[tuple(spot)].set(low)
    longest = shape.index(max(shape))
    spot[longest] = (spot[longest] + 1) % shape[longest]
    return result.at[tuple(spot)].set(largest)


def level_of(key, extent, pieces, low, high):
    factor_of, own = 1.0, jax.random.fold_in(key, 6)
    for dim, shards_of in pieces:
        heights = jnp.exp(jax.random.uniform(jax.random.fold_in(own, dim), (shards_of,), jnp.float32, low / len(pieces), high / len(pieces)))
        factor_of = factor_of * jnp.repeat(heights, extent[dim] // shards_of).reshape([-1 if axis == dim else 1 for axis in range(len(extent))])
    return factor_of


def split_up(amount, total, most, slope):
    portions = [(1 << 20) // math.isqrt(standing ** slope) + 1 for standing in range(2, amount + 1)]
    spare, given = total - most - (amount - 1), [1] * (amount - 1)
    while spare > 0:
        movable = [i for i in range(amount - 1) if given[i] < most]
        mass, remaining = sum([portions[i] for i in movable]), spare
        for i in movable:
            more = min(most - given[i], max(1, remaining * portions[i] // mass), spare)
            given[i] = given[i] + more
            spare = spare - more
    return np.array([most] + given)


def uneven(rng, amount, total, reach, skew):
    if amount == 2:
        one = jax.random.randint(rng, (), max(1, total - reach), min(reach, total - 1) + 1)
        return jnp.stack([one, total - one])
    tallies = jnp.asarray(split_up(amount, total, reach, skew), jnp.int32)
    couples = (amount - 1) // 2
    source_of, receiver = tallies[1:1 + 2 * couples:2], tallies[2:2 + 2 * couples:2]
    slack = jnp.minimum(source_of - 1, reach - receiver)
    shifted = jax.random.randint(jax.random.fold_in(rng, 1), (couples,), 0, 1 << 20) % (slack + 1)
    tallies = tallies.at[1:1 + 2 * couples:2].set(source_of - shifted).at[2:2 + 2 * couples:2].set(receiver + shifted)
    return tallies[jax.random.permutation(jax.random.fold_in(rng, 2), amount)]


def centred(own_key, shape, width, most, pieces=(), kind=jnp.bfloat16):
    values = jax.random.normal(own_key, shape, jnp.float32) * width
    if len(pieces) > 0:
        values = level_of(own_key, shape, pieces, -0.22, 0.18) * values
    return jnp.clip(values, min=-most, max=most).astype(kind)


def setup_inputs(seed: int = 0) -> dict:
    key_list = jax.random.split(jax.random.key(seed), 8)
    flow_field = centred(key_list[0], (4, GX, GY, GZ), 1.0, 6.0, ((1, 64), (2, 8)), jnp.float32)
    disk_mask = place_ends((jax.random.randint(key_list[1], (GX, GY, GZ), 0, 4) < 1).astype(jnp.int32), jax.random.fold_in(key_list[1], 1), 0, 1)
    surf_cell = place_ends(jax.random.randint(key_list[2], (N_OBS, N_CFD * PMAX), 0, CX * CY * CZ), jax.random.fold_in(key_list[2], 1), 0, (CX * CY * CZ) - 1).astype(jnp.int32)
    delay_bin = place_ends(jax.random.randint(key_list[3], (N_OBS, N_CFD * PMAX), 0, SAMPLES - STEPS - 2), jax.random.fold_in(key_list[3], 1), 0, (SAMPLES - STEPS - 2) - 1).astype(jnp.int32)
    tap_phase = place_ends(jax.random.randint(key_list[4], (N_OBS, N_CFD * PMAX), 0, 4), jax.random.fold_in(key_list[4], 1), 0, 3).astype(jnp.int32)
    panel_counts = jax.vmap(lambda own: uneven(own, N_CFD, PAN_COL, PMAX, 2))(jax.random.split(key_list[5], N_OBS)).reshape((N_OBS, N_CFD)).astype(jnp.int32)
    observer_pos = jnp.clip(1.0 * jax.random.uniform(key_list[6], (3, OBSERVERS), jnp.float32) ** level_of(key_list[6], (3, OBSERVERS), ((1, 64),), -0.2, 0.2), 0.0, 1.0)
    return {"flow_field": flow_field, "disk_mask": disk_mask, "surf_cell": surf_cell, "delay_bin": delay_bin, "tap_phase": tap_phase, "panel_counts": panel_counts, "observer_pos": observer_pos}


def advance(state, padded, mask_float):
    x_plus = padded[:, 2:, 1:-1, 1:-1]
    x_minus = padded[:, :-2, 1:-1, 1:-1]
    y_plus = padded[:, 1:-1, 2:, 1:-1]
    y_minus = padded[:, 1:-1, :-2, 1:-1]
    z_plus = padded[:, 1:-1, 1:-1, 2:]
    z_minus = padded[:, 1:-1, 1:-1, :-2]
    laplace = x_plus + x_minus + y_plus + y_minus + z_plus + z_minus - 6.0 * state
    moved = state + 0.1 * laplace + 0.3 * (x_minus - state)
    pressure = moved[0] + 0.5 * mask_float * state[1]
    velocity = moved[1:] - 0.4 * mask_float[None] * state[1:]
    return jnp.concatenate([pressure[None], velocity], axis=0)

def lagrange(phase):
    frac = phase * 0.25
    return [-frac * (frac - 1.0) * (frac - 2.0) / 6.0, (frac + 1.0) * (frac - 1.0) * (frac - 2.0) / 2.0, -(frac + 1.0) * frac * (frac - 2.0) / 2.0, (frac + 1.0) * frac * (frac - 1.0) / 6.0]

def contribution(record, targets):
    steps_count = (record.shape[0] - 5) // 4
    values = record[:4 * steps_count]
    places = record[4 * steps_count:4 * steps_count + 3]
    delays = record[4 * steps_count + 3]
    weights = lagrange(record[4 * steps_count + 4])
    offset = jnp.arange(SAMPLES, dtype=jnp.float32)[None, :] - delays[:, None]
    banded = jnp.zeros((4, record.shape[1], SAMPLES), jnp.float32)
    for lag in range(steps_count + 3):
        summed = jnp.zeros((4, record.shape[1]), jnp.float32)
        for step in range(steps_count):
            tap = lag - step
            if 0 <= tap <= 3:
                summed = summed + values[4 * step:4 * step + 4] * weights[tap][None]
        banded = banded + jnp.where((offset == lag)[None], summed[:, :, None], 0.0)
    apart = targets[:, :, None] - places[:, None, :]
    squared = apart[0] * apart[0] + apart[1] * apart[1] + apart[2] * apart[2] + 16.0
    radius = jnp.sqrt(squared)
    inverse = 4.0 / radius
    kernel = jnp.stack([inverse, inverse * apart[0] / radius, inverse * apart[1] / radius, inverse * apart[2] / radius], axis=0)
    return (kernel.astype(jnp.bfloat16), banded.astype(jnp.bfloat16))

def reference(flow_field, disk_mask, surf_cell, delay_bin, tap_phase, panel_counts, observer_pos):
    mask_float = disk_mask.astype(jnp.float32)
    block_col = (jnp.arange(N_CFD * PMAX, dtype=jnp.int32) // PMAX)[None, :]
    row_index = jnp.arange(N_OBS, dtype=jnp.int32)[:, None]
    glob_x = block_col * CX + surf_cell // (CY * CZ)
    glob_y = row_index * CY + surf_cell // CZ % CY
    glob_z = surf_cell % CZ
    state = flow_field
    sampled = []
    for step in range(STEPS):
        padded = jnp.pad(state, ((0, 0), (1, 1), (1, 1), (1, 1)))
        state = advance(state, padded, mask_float)
        sampled.append(state[:, glob_x, glob_y, glob_z])
    extras = [glob_x.astype(jnp.float32)[None] + 0.5, glob_y.astype(jnp.float32)[None] + 0.5, glob_z.astype(jnp.float32)[None] + 0.5, delay_bin.astype(jnp.float32)[None], tap_phase.astype(jnp.float32)[None]]
    record = jnp.concatenate(sampled + extras, axis=0)
    ends = jnp.cumsum(panel_counts, axis=1).astype(jnp.int32)
    position = jnp.arange(PAN_COL, dtype=jnp.int32)
    source = lax.optimization_barrier(jnp.sum((ends[:, None, :] <= position[None, :, None]).astype(jnp.int32), axis=2)).astype(jnp.int32)
    starts = jnp.take_along_axis(ends - panel_counts, source, axis=1).astype(jnp.int32)
    slot_index = (source * PMAX + position[None, :] - starts).astype(jnp.int32)
    fields = record.shape[0]
    compact = jnp.take_along_axis(record, jnp.broadcast_to(slot_index[None], (fields, N_OBS, PAN_COL)), axis=2)
    compact = compact.reshape(fields, N_OBS * PAN_COL)
    targets = observer_pos * jnp.array([GX, GY, GZ], jnp.float32)[:, None]
    block_size = math.gcd(N_OBS * PAN_COL, 1024)
    blocks = compact.reshape(fields, N_OBS * PAN_COL // block_size, block_size).transpose(1, 0, 2)

    def add_block(running, segment):
        kernel, banded = contribution(segment, targets)
        product = jnp.einsum('cop,cpt->ot', kernel.astype(jnp.float32), banded.astype(jnp.float32))
        return (running + product, None)
    signal, _ = lax.scan(add_block, jnp.zeros((OBSERVERS, SAMPLES), jnp.float32), blocks)
    return (state, signal)
```

```python
import functools

import jax
import jax.numpy as jnp
from jax import lax
from jax.experimental import pallas as pl
from jax.experimental.pallas import tpu as pltpu
from jax.sharding import PartitionSpec as P

STEPS = 4
SAMPLES = 512
SLOTS = 128
TARGETS = 128
CHUNK = 4
MESH = pl.DeviceIdType.MESH
F32 = jnp.float32
BF16 = jnp.bfloat16


def kernel(
    rings,
    flow,
    disk,
    cells,
    delays,
    phases,
    counts,
    spots,
    flow_out,
    signal,
    state,
    x_halo,
    y_halo,
    y_face,
    meta,
    values,
    onehot,
    towards,
    greens,
    bands,
    sums,
    whole,
    parts,
    x_send,
    x_recv,
    y_send,
    y_recv,
    meta_z_send,
    meta_z_recv,
    meta_y_send,
    meta_y_recv,
    val_z_send,
    val_z_recv,
    val_y_send,
    val_y_recv,
    part_send,
    part_recv,
):
    n_y, n_z, n_obs = rings
    n_cfd = n_y * n_z
    cfd = lax.axis_index("cfd")
    obs = lax.axis_index("obs")
    here_y = cfd // n_z
    here_z = cfd % n_z
    size_x, size_y, size_z = flow.shape[1:]
    owned = TARGETS // n_obs

    def along_z(far):
        return here_y * n_z + lax.rem(here_z + far, n_z)

    def along_y(far):
        return lax.rem(here_y + far, n_y) * n_z + here_z

    def along_obs(far):
        return lax.rem(obs + far, n_obs)

    cfd_next, cfd_prev = lax.rem(cfd + 1, n_cfd), lax.rem(cfd + n_cfd - 1, n_cfd)
    obs_next, obs_prev = along_obs(1), along_obs(n_obs - 1)

    barrier = pltpu.get_barrier_semaphore()

    def greet(to_cfd, to_obs):
        pl.semaphore_signal(barrier, inc=1, device_id=(to_cfd, to_obs), device_id_type=MESH)

    for far in range(1, n_z):
        greet(along_z(far), obs)
    for far in range(1, n_y):
        greet(along_y(far), obs)
    for far in range(1, n_obs):
        greet(cfd, along_obs(far))
    greet(cfd_next, obs)
    greet(cfd_prev, obs)

    cell = cells[...]
    row_of = cell >> 7
    z_of = cell & 127
    phase = phases[...].astype(F32) * 0.25
    live_at = (lax.broadcasted_iota(jnp.int32, counts.shape, 0) == obs) & (
        lax.broadcasted_iota(jnp.int32, counts.shape, 1) == cfd
    )
    own = jnp.sum(jnp.where(live_at, counts[...], 0).astype(F32), axis=(0, 1), keepdims=True)
    live = lax.broadcasted_iota(jnp.int32, (1, SLOTS), 1).astype(F32) < own
    meta[cfd] = jnp.concatenate(
        [
            (cfd * size_x + (cell >> 11)).astype(F32) + 0.5,
            (obs * size_y + (row_of & 15)).astype(F32) + 0.5,
            z_of.astype(F32) + 0.5,
            delays[...].astype(F32),
            -phase * (phase - 1.0) * (phase - 2.0) / 6.0,
            (phase + 1.0) * (phase - 1.0) * (phase - 2.0) / 2.0,
            -(phase + 1.0) * phase * (phase - 2.0) / 2.0,
            (phase + 1.0) * phase * (phase - 1.0) / 6.0,
        ],
        axis=0,
    )
    onehot[...] = jnp.where(
        lax.broadcasted_iota(jnp.int32, (size_x * size_y, SLOTS), 0) == row_of, 1.0, 0.0
    ).astype(BF16)
    z_at = lax.broadcasted_iota(jnp.int32, (size_z, SLOTS), 0) == z_of

    row = lax.broadcasted_iota(jnp.int32, (size_y, size_z), 0)
    lane = lax.broadcasted_iota(jnp.int32, (size_y, size_z), 1)

    def fields(step):
        if step == 0:
            return flow
        return flow_out if step == STEPS else state.at[step - 1]

    def x_copy(step, side):
        edge = size_x - 1 if side == 0 else 0
        return pltpu.make_async_remote_copy(
            src_ref=fields(step).at[:, edge],
            dst_ref=x_halo.at[step, side],
            send_sem=x_send.at[step, side],
            recv_sem=x_recv.at[step, side],
            device_id=(cfd_next if side == 0 else cfd_prev, obs),
            device_id_type=MESH,
        )

    def y_copy(step, side):
        return pltpu.make_async_remote_copy(
            src_ref=y_face.at[step, side],
            dst_ref=y_halo.at[step, side],
            send_sem=y_send.at[step, side],
            recv_sem=y_recv.at[step, side],
            device_id=(cfd, obs_next if side == 0 else obs_prev),
            device_id_type=MESH,
        )

    def halo_start(step):
        for side in range(2):
            y_copy(step, side).start()
            x_copy(step, side).start()

    def halo_wait(step):
        for side in range(2):
            y_copy(step, side).wait()
            x_copy(step, side).wait()

    def faces(step):
        ref = fields(step)

        @pl.loop(0, size_x)
        def _(i):
            for c in range(4):
                y_face[step, 0, c, pl.ds(i, 1), :] = ref[c, i, size_y - 1 : size_y, :]
                y_face[step, 1, c, pl.ds(i, 1), :] = ref[c, i, 0:1, :]

    def main(step):
        ref, new = fields(step), fields(step + 1)

        @pl.loop(0, size_x)
        def _(i):
            disk_here = disk[i].astype(F32)
            below = jnp.where(i > 0, 0.4, 0.0)
            above = jnp.where(i < size_x - 1, 0.1, 0.0)
            before = jnp.maximum(i - 1, 0)
            after = jnp.minimum(i + 1, size_x - 1)
            slabs = [ref[c, i] for c in range(4)]
            for c in range(4):
                q = slabs[c]
                near = (
                    q
                    + jnp.where(row == 0, 0.0, pltpu.roll(q, 1, 0))
                    + jnp.where(row == size_y - 1, 0.0, pltpu.roll(q, size_y - 1, 0))
                    + jnp.where(lane == 0, 0.0, pltpu.roll(q, 1, 1))
                    + jnp.where(lane == size_z - 1, 0.0, pltpu.roll(q, size_z - 1, 1))
                )
                moved = 0.1 * near + below * ref[c, before] + above * ref[c, after]
                pull = 0.5 * slabs[1] if c == 0 else -0.4 * q
                new[c, i] = moved + disk_here * pull

    def fix(step):
        new = fields(step + 1)
        x_low = jnp.where(cfd > 0, 0.4, 0.0)
        x_high = jnp.where(cfd < n_cfd - 1, 0.1, 0.0)
        y_low = jnp.where(obs > 0, 0.1, 0.0)
        y_high = jnp.where(obs < n_obs - 1, 0.1, 0.0)
        for c in range(4):
            new[c, 0] = new[c, 0] + x_low * x_halo[step, 0, c]
            new[c, size_x - 1] = new[c, size_x - 1] + x_high * x_halo[step, 1, c]

        @pl.loop(0, size_x)
        def _(i):
            for c in range(4):
                low = y_low * y_halo[step, 0, c, pl.ds(i, 1), :]
                high = y_high * y_halo[step, 1, c, pl.ds(i, 1), :]
                slab = new[c, i] + jnp.where(
                    row == 0, low, jnp.where(row == size_y - 1, high, 0.0)
                )
                new[c, i] = slab
                if step + 1 < STEPS:
                    y_face[step + 1, 0, c, pl.ds(i, 1), :] = slab[size_y - 1 : size_y]
                    y_face[step + 1, 1, c, pl.ds(i, 1), :] = slab[0:1]

    def sample(step):
        new = fields(step + 1)
        for c in range(4):
            q = new[c].reshape(size_x * size_y, size_z)
            high = q.astype(BF16)
            low = (q - high.astype(F32)).astype(BF16)
            dims = (((0,), (0,)), ((), ()))
            lines = lax.dot_general(high, onehot[...], dims, preferred_element_type=F32)
            lines = lines + lax.dot_general(low, onehot[...], dims, preferred_element_type=F32)
            v = jnp.sum(jnp.where(z_at, lines, 0.0), axis=0, keepdims=True)
            values[step, cfd, c : c + 1, :] = jnp.where(live, v, 0.0)

    def z_copy(buf, block, send, recv, far, source):
        return pltpu.make_async_remote_copy(
            src_ref=buf.at[block],
            dst_ref=buf.at[block],
            send_sem=send.at[far],
            recv_sem=recv.at[source],
            device_id=(along_z(far), obs),
            device_id_type=MESH,
        )

    def z_start(buf, send, recv):
        @pl.loop(1, n_z)
        def _(far):
            z_copy(buf, cfd, send, recv, far, far).start()

    def z_wait(buf, send, recv):
        @pl.loop(1, n_z)
        def _(far):
            z_copy(buf, cfd, send, recv, far, far).wait_send()
            source = here_y * n_z + lax.rem(here_z + n_z - far, n_z)
            z_copy(buf, source, send, recv, far, far).wait_recv()

    def y_group(buf, group, send, recv, far):
        block = pl.ds(pl.multiple_of(group * n_z, n_z), n_z)
        return pltpu.make_async_remote_copy(
            src_ref=buf.at[block],
            dst_ref=buf.at[block],
            send_sem=send.at[far],
            recv_sem=recv.at[far],
            device_id=(along_y(far), obs),
            device_id_type=MESH,
        )

    def group_at(back):
        return lax.rem(here_y + n_y - back, n_y)

    def y_start(buf, send, recv):
        for far in range(1, n_y):
            y_group(buf, here_y, send, recv, far).start()

    def y_wait_recv(buf, send, recv, far):
        y_group(buf, group_at(far), send, recv, far).wait_recv()

    def y_wait_send(buf, send, recv):
        for far in range(1, n_y):
            y_group(buf, here_y, send, recv, far).wait_send()

    def prepare(group):
        @pl.loop(0, n_z)
        def _(k):
            block = group * n_z + k
            rows = meta[block]
            for first in range(0, TARGETS, 32):
                part = pl.ds(first, 32)
                d = [towards[a, part, :] - rows[a : a + 1] for a in range(3)]
                inv = lax.rsqrt(d[0] * d[0] + d[1] * d[1] + d[2] * d[2] + 16.0)
                four = 4.0 * inv
                square = four * inv
                greens[block, 0, part, :] = four
                for a in range(3):
                    greens[block, a + 1, part, :] = square * d[a]
            for first in range(0, SAMPLES, 64):
                at = (lax.broadcasted_iota(jnp.int32, (64, SLOTS), 0) + first).astype(F32)
                band = jnp.zeros((64, SLOTS), F32)
                for tap in range(4):
                    band = jnp.where(at == rows[3:4] + float(tap), rows[4 + tap : 5 + tap], band)
                bands[block, pl.ds(first, 64), :] = band.astype(BF16)

    def radiate(group, steps):
        many = min(CHUNK, n_z)

        @pl.loop(0, n_z // many)
        def _(k):
            start = group * n_z + k * many
            lhs = jnp.concatenate([bands[start + j] for j in range(many)], axis=1)
            columns = []
            for j in range(many):
                pieces = []
                for step in steps:
                    v = values[step, start + j]
                    for first in range(0, TARGETS, 32):
                        part = pl.ds(first, 32)
                        term = greens[start + j, 0, part, :] * v[0:1]
                        for c in range(1, 4):
                            term = term + greens[start + j, c, part, :] * v[c : c + 1]
                        pieces.append(term.astype(BF16))
                columns.append(jnp.concatenate(pieces, axis=0))
            rhs = jnp.concatenate(columns, axis=1)
            out = lax.dot_general(lhs, rhs, (((1,), (1,)), ((), ())), preferred_element_type=F32)
            for at, step in enumerate(steps):
                sums[step] += out[:, at * TARGETS : (at + 1) * TARGETS]

    def meta_refs():
        return (meta, meta_z_send, meta_z_recv)

    def meta_y_refs():
        return (meta, meta_y_send, meta_y_recv)

    def val_refs(step):
        return (values.at[step], val_z_send.at[step], val_z_recv.at[step])

    def val_y_refs(step):
        return (values.at[step], val_y_send.at[step], val_y_recv.at[step])

    faces(0)
    pl.semaphore_wait(barrier, n_z - 1 + n_y - 1 + n_obs - 1 + 2)

    halo_start(0)
    z_start(*meta_refs())
    extent = (size_x * n_cfd, size_y * n_obs, size_z)
    for a in range(3):
        line = spots[a : a + 1] * float(extent[a])
        towards[a] = jnp.transpose(jnp.broadcast_to(line, (SLOTS, TARGETS)))
    sums[...] = jnp.zeros_like(sums)
    main(0)
    halo_wait(0)
    fix(0)
    halo_start(1)
    sample(0)
    z_start(*val_refs(0))
    main(1)
    z_wait(*meta_refs())
    y_start(*meta_y_refs())
    prepare(here_y)
    halo_wait(1)
    fix(1)
    halo_start(2)
    sample(1)
    z_start(*val_refs(1))
    main(2)
    z_wait(*val_refs(0))
    y_start(*val_y_refs(0))
    if n_y > 1:
        y_wait_recv(*meta_y_refs(), 1)
        prepare(group_at(1))
    halo_wait(2)
    fix(2)
    halo_start(3)
    sample(2)
    z_start(*val_refs(2))
    main(3)
    z_wait(*val_refs(1))
    y_start(*val_y_refs(1))
    if n_y > 2:
        y_wait_recv(*meta_y_refs(), 2)
        prepare(group_at(2))
    halo_wait(3)
    fix(3)
    sample(3)
    z_start(*val_refs(3))
    z_wait(*val_refs(2))
    y_start(*val_y_refs(2))
    for far in range(3, n_y):
        y_wait_recv(*meta_y_refs(), far)
        prepare(group_at(far))
    z_wait(*val_refs(3))
    y_start(*val_y_refs(3))
    y_wait_send(*meta_y_refs())
    for far in range(n_y):
        if far > 0:
            y_wait_recv(*val_y_refs(0), far)
            y_wait_recv(*val_y_refs(1), far)
        radiate(group_at(far), (0, 1))
    for far in range(n_y):
        if far > 0:
            y_wait_recv(*val_y_refs(2), far)
            y_wait_recv(*val_y_refs(3), far)
        radiate(group_at(far), (2, 3))
    for step in range(STEPS):
        y_wait_send(*val_y_refs(step))

    total = sums[0]
    for step in range(1, STEPS):
        total = total + pltpu.roll(sums[step], step, 0)
    whole[...] = jnp.transpose(total)

    def part_copy(far):
        return pltpu.make_async_remote_copy(
            src_ref=whole.at[pl.ds(pl.multiple_of(along_obs(far) * owned, owned), owned)],
            dst_ref=parts.at[far - 1],
            send_sem=part_send.at[far - 1],
            recv_sem=part_recv.at[far - 1],
            device_id=(cfd, along_obs(far)),
            device_id_type=MESH,
        )

    for far in range(1, n_obs):
        part_copy(far).start()
    result = whole[pl.ds(pl.multiple_of(obs * owned, owned), owned), :]
    for far in range(1, n_obs):
        part_copy(far).wait()
        result = result + parts[far - 1]
    signal[...] = result


def per_device(rings, flow_field, disk_mask, surf_cell, delay_bin, tap_phase, panel_counts, observer_pos):
    n_y, n_z, n_obs = rings
    n_cfd = n_y * n_z
    _, size_x, size_y, size_z = flow_field.shape
    owned = TARGETS // n_obs
    dma = pltpu.SemaphoreType.DMA
    vmem = pl.BlockSpec(memory_space=pltpu.VMEM)
    return pl.pallas_call(
        functools.partial(kernel, rings),
        out_shape=(
            jax.ShapeDtypeStruct(flow_field.shape, F32),
            jax.ShapeDtypeStruct((owned, SAMPLES), F32),
        ),
        in_specs=[vmem] * 7,
        out_specs=(vmem, vmem),
        scratch_shapes=[
            pltpu.VMEM((STEPS - 1,) + flow_field.shape, F32),
            pltpu.VMEM((STEPS, 2, 4, size_y, size_z), F32),
            pltpu.VMEM((STEPS, 2, 4, size_x, size_z), F32),
            pltpu.VMEM((STEPS, 2, 4, size_x, size_z), F32),
            pltpu.VMEM((n_cfd, 8, SLOTS), F32),
            pltpu.VMEM((STEPS, n_cfd, 4, SLOTS), F32),
            pltpu.VMEM((size_x * size_y, SLOTS), BF16),
            pltpu.VMEM((3, TARGETS, SLOTS), F32),
            pltpu.VMEM((n_cfd, 4, TARGETS, SLOTS), F32),
            pltpu.VMEM((n_cfd, SAMPLES, SLOTS), BF16),
            pltpu.VMEM((STEPS, SAMPLES, TARGETS), F32),
            pltpu.VMEM((TARGETS, SAMPLES), F32),
            pltpu.VMEM((n_obs - 1, owned, SAMPLES), F32),
            dma((STEPS, 2)),
            dma((STEPS, 2)),
            dma((STEPS, 2)),
            dma((STEPS, 2)),
            dma((n_z,)),
            dma((n_z,)),
            dma((n_y,)),
            dma((n_y,)),
            dma((STEPS, n_z)),
            dma((STEPS, n_z)),
            dma((STEPS, n_y)),
            dma((STEPS, n_y)),
            dma((n_obs - 1,)),
            dma((n_obs - 1,)),
        ],
        compiler_params=pltpu.CompilerParams(
            collective_id=0, has_side_effects=True, vmem_limit_bytes=48 * 1024 * 1024
        ),
    )(flow_field, disk_mask, surf_cell, delay_bin, tap_phase, panel_counts, observer_pos)


def solution(mesh):
    n_cfd, n_obs = mesh.shape["cfd"], mesh.shape["obs"]
    n_y = 4 if n_cfd >= 16 else 2
    rings = (n_y, n_cfd // n_y, n_obs)
    return jax.shard_map(
        functools.partial(per_device, rings),
        mesh=mesh,
        in_specs=(
            P(None, "cfd", "obs", None),
            P("cfd", "obs", None),
            P("obs", "cfd"),
            P("obs", "cfd"),
            P("obs", "cfd"),
            P(),
            P(None, "cfd"),
        ),
        out_specs=(P(None, "cfd", "obs", None), P(("cfd", "obs"), None)),
        check_vma=False,
    )
```

```python
import functools

import jax
import jax.numpy as jnp
from jax import lax
from jax.experimental import pallas as pl
from jax.experimental.pallas import tpu as pltpu
from jax.sharding import PartitionSpec as P

STEPS = 4
SAMPLES = 512
SLOTS = 128
TARGETS = 128
WIDTH = 4
SIDE = 8
MESH = pl.DeviceIdType.MESH
F32 = jnp.float32
BF16 = jnp.bfloat16


def kernel(
    rings,
    flow_in,
    disk_in,
    cells_in,
    delays_in,
    phases_in,
    counts_in,
    spots_in,
    flow_out,
    signal,
    disk,
    cells,
    delays,
    phases,
    counts,
    spots,
    in_sem,
    wide,
    state,
    last,
    meta,
    values,
    onehot,
    towards,
    greens,
    bands,
    sums,
    whole,
    parts,
    halo_send,
    halo_recv,
    meta_z_send,
    meta_z_recv,
    meta_y_send,
    meta_y_recv,
    val_z_send,
    val_z_recv,
    val_y_send,
    val_y_recv,
    part_send,
    part_recv,
):
    n_y, n_z, n_obs = rings
    n_cfd = n_y * n_z
    cfd = lax.axis_index("cfd")
    obs = lax.axis_index("obs")
    here_y = cfd // n_z
    here_z = cfd % n_z
    size_x, size_y, size_z = flow_in.shape[1:]
    owned = TARGETS // n_obs
    own_x = slice(WIDTH, WIDTH + size_x)
    own_y = slice(SIDE, SIDE + size_y)
    tall = size_y + 2 * SIDE

    def along_z(far):
        return here_y * n_z + lax.rem(here_z + far, n_z)

    def along_y(far):
        return lax.rem(here_y + far, n_y) * n_z + here_z

    def along_obs(far):
        return lax.rem(obs + far, n_obs)

    cfd_next, cfd_prev = lax.rem(cfd + 1, n_cfd), lax.rem(cfd + n_cfd - 1, n_cfd)
    obs_next, obs_prev = along_obs(1), along_obs(n_obs - 1)

    inputs = [
        pltpu.make_async_copy(src, dst, in_sem.at[i])
        for i, (src, dst) in enumerate(
            [
                (disk_in, disk),
                (flow_in, wide.at[0:4, own_x, own_y]),
                (cells_in, cells),
                (delays_in, delays),
                (phases_in, phases),
                (counts_in, counts),
                (spots_in, spots),
            ]
        )
    ]
    for copy in inputs:
        copy.start()

    barrier = pltpu.get_barrier_semaphore()

    def greet(to_cfd, to_obs):
        pl.semaphore_signal(barrier, inc=1, device_id=(to_cfd, to_obs), device_id_type=MESH)

    for to_cfd in (cfd_next, cfd_prev):
        for to_obs in (obs_next, obs_prev, obs):
            greet(to_cfd, to_obs)
    for far in range(1, n_z):
        greet(along_z(far), obs)
    for far in range(1, n_y):
        greet(along_y(far), obs)
    for far in range(1, n_obs):
        greet(cfd, along_obs(far))

    inputs[0].wait()
    for i in range(size_x):
        wide[4, WIDTH + i, own_y] = disk[i].astype(F32)
    for copy in inputs[1:]:
        copy.wait()

    cell = cells[...]
    row_of = cell >> 7
    live_at = (lax.broadcasted_iota(jnp.int32, counts.shape, 0) == obs) & (
        lax.broadcasted_iota(jnp.int32, counts.shape, 1) == cfd
    )
    own = jnp.sum(jnp.where(live_at, counts[...], 0).astype(F32), axis=(0, 1), keepdims=True)
    live = lax.broadcasted_iota(jnp.int32, (1, SLOTS), 1).astype(F32) < own
    meta[cfd] = jnp.concatenate(
        [
            cell.astype(F32),
            delays[...].astype(F32),
            phases[...].astype(F32),
            jnp.zeros((1, SLOTS), F32),
        ],
        axis=0,
    )
    pl.semaphore_wait(barrier, 6 + n_z - 1 + n_y - 1 + n_obs - 1)

    def halo_copies():
        low_x, high_x = slice(0, WIDTH), slice(WIDTH + size_x, 2 * WIDTH + size_x)
        low_y, high_y = slice(0, SIDE), slice(SIDE + size_y, tall)
        first_x, last_x = slice(WIDTH, 2 * WIDTH), slice(size_x, size_x + WIDTH)
        first_y, last_y = slice(SIDE, 2 * SIDE), slice(size_y, size_y + SIDE)
        low_c, high_c = slice(1, WIDTH), slice(WIDTH + size_x, 2 * WIDTH + size_x - 1)
        first_c, last_c = slice(WIDTH, 2 * WIDTH - 1), slice(size_x + 1, size_x + WIDTH)
        moves = [
            (last_x, own_y, low_x, own_y, cfd_next, obs),
            (first_x, own_y, high_x, own_y, cfd_prev, obs),
            (last_c, last_y, low_c, low_y, cfd_next, obs_next),
            (last_c, first_y, low_c, high_y, cfd_next, obs_prev),
            (first_c, last_y, high_c, low_y, cfd_prev, obs_next),
            (first_c, first_y, high_c, high_y, cfd_prev, obs_prev),
            (own_x, last_y, own_x, low_y, cfd, obs_next),
            (own_x, first_y, own_x, high_y, cfd, obs_prev),
        ]
        return [
            pltpu.make_async_remote_copy(
                src_ref=wide.at[:, from_x, from_y],
                dst_ref=wide.at[:, to_x, to_y],
                send_sem=halo_send.at[i],
                recv_sem=halo_recv.at[i],
                device_id=(to_cfd, to_obs),
                device_id_type=MESH,
            )
            for i, (from_x, from_y, to_x, to_y, to_cfd, to_obs) in enumerate(moves)
        ]

    def fields(step):
        return wide if step == 0 else state.at[step - 1]

    def outside(step):
        ref = fields(step)

        @pl.when(cfd == 0)
        def _():
            ref[0:4, 0:WIDTH] = jnp.zeros((4, WIDTH, tall, size_z), F32)

        @pl.when(cfd == n_cfd - 1)
        def _():
            ref[0:4, WIDTH + size_x :] = jnp.zeros((4, WIDTH, tall, size_z), F32)

        @pl.when(obs == 0)
        def _():
            ref[0:4, :, 0:SIDE] = jnp.zeros((4, size_x + 2 * WIDTH, SIDE, size_z), F32)

        @pl.when(obs == n_obs - 1)
        def _():
            ref[0:4, :, SIDE + size_y :] = jnp.zeros((4, size_x + 2 * WIDTH, SIDE, size_z), F32)

    lane = lax.broadcasted_iota(jnp.int32, (tall, size_z), 1)

    def advance(step):
        ref = fields(step)
        final = step == STEPS - 1

        @pl.loop(1 + step, 2 * WIDTH + size_x - 1 - step, unroll=True)
        def _(i):
            slabs = [ref[c, i] for c in range(4)]
            there = wide[4, i]
            for c in range(4):
                q = slabs[c]
                near = (
                    q
                    + ref[c, i + 1]
                    + pltpu.roll(q, 1, 0)
                    + pltpu.roll(q, tall - 1, 0)
                    + jnp.where(lane == 0, 0.0, pltpu.roll(q, 1, 1))
                    + jnp.where(lane == size_z - 1, 0.0, pltpu.roll(q, size_z - 1, 1))
                )
                pull = 0.5 * slabs[1] if c == 0 else -0.4 * q
                moved = 0.1 * near + 0.4 * ref[c, i - 1] + there * pull
                if final:
                    last[c, i - WIDTH] = moved[own_y]
                else:
                    state[step, c, i] = moved

    def sample(step):
        for c in range(4):
            block = last[c] if step == STEPS - 1 else state[step, c, own_x, own_y]
            q = block.reshape(size_x * size_y, size_z)
            high = q.astype(BF16)
            low = (q - high.astype(F32)).astype(BF16)
            dims = (((0,), (0,)), ((), ()))
            lines = lax.dot_general(high, onehot[...], dims, preferred_element_type=F32)
            lines = lines + lax.dot_general(low, onehot[...], dims, preferred_element_type=F32)
            z_at = lax.broadcasted_iota(jnp.int32, (size_z, SLOTS), 0) == (cells[...] & 127)
            v = jnp.sum(jnp.where(z_at, lines, 0.0), axis=0, keepdims=True)
            values[step, cfd, c : c + 1, :] = jnp.where(live, v, 0.0)

    def z_copy(buf, block, send, recv, far, source):
        return pltpu.make_async_remote_copy(
            src_ref=buf.at[block],
            dst_ref=buf.at[block],
            send_sem=send.at[far],
            recv_sem=recv.at[source],
            device_id=(along_z(far), obs),
            device_id_type=MESH,
        )

    def z_start(buf, send, recv):
        @pl.loop(0, n_z - 1)
        def _(k):
            far = 1 + lax.rem(k + n_z // 2 - 1, n_z - 1)
            z_copy(buf, cfd, send, recv, far, far).start()

    def z_wait(buf, send, recv):
        @pl.loop(1, n_z)
        def _(far):
            source = here_y * n_z + lax.rem(here_z + n_z - far, n_z)
            z_copy(buf, source, send, recv, far, far).wait_recv()

    def z_wait_send(buf, send, recv):
        @pl.loop(1, n_z)
        def _(far):
            z_copy(buf, cfd, send, recv, far, far).wait_send()

    def y_group(buf, group, send, recv, far):
        block = pl.ds(pl.multiple_of(group * n_z, n_z), n_z)
        return pltpu.make_async_remote_copy(
            src_ref=buf.at[block],
            dst_ref=buf.at[block],
            send_sem=send.at[far],
            recv_sem=recv.at[far],
            device_id=(along_y(far), obs),
            device_id_type=MESH,
        )

    def group_at(back):
        return lax.rem(here_y + n_y - back, n_y)

    def y_start(buf, send, recv):
        for far in range(1, n_y):
            y_group(buf, here_y, send, recv, far).start()

    def y_wait_recv(buf, send, recv, far):
        y_group(buf, group_at(far), send, recv, far).wait_recv()

    def y_wait_send(buf, send, recv):
        for far in range(1, n_y):
            y_group(buf, here_y, send, recv, far).wait_send()

    def prepare(group):
        at = lax.broadcasted_iota(jnp.int32, (16, SLOTS), 0).astype(F32)
        none = jnp.zeros((16, SLOTS), BF16)

        @pl.loop(0, n_z, unroll=4)
        def _(k):
            block = group * n_z + k
            rows = meta[block]
            where = rows[0:1]
            slab = jnp.floor(where * (1.0 / (size_y * size_z)))
            inner = where - float(size_y * size_z) * slab
            line = jnp.floor(inner * (1.0 / size_z))
            place = [
                slab + ((block * size_x).astype(F32) + 0.5),
                line + ((obs * size_y).astype(F32) + 0.5),
                inner - float(size_z) * line + 0.5,
            ]
            delay = rows[1:2]
            frac = rows[2:3] * 0.25
            weights = [
                -frac * (frac - 1.0) * (frac - 2.0) / 6.0,
                (frac + 1.0) * (frac - 1.0) * (frac - 2.0) * 0.5,
                -(frac + 1.0) * frac * (frac - 2.0) * 0.5,
                (frac + 1.0) * frac * (frac - 1.0) / 6.0,
            ]
            high = jnp.floor(delay * 0.0625)
            low = delay - 16.0 * high
            first, second = jnp.zeros((16, SLOTS), F32), jnp.zeros((16, SLOTS), F32)
            for tap in range(4):
                first = jnp.where(at == low + float(tap), weights[tap], first)
                second = jnp.where(at + 16.0 == low + float(tap), weights[tap], second)
            first, second = first.astype(BF16), second.astype(BF16)
            high = jnp.broadcast_to(high, (16, SLOTS)).astype(BF16)
            before = None
            for part in range(SAMPLES // 16):
                here = high == jnp.asarray(float(part), BF16)
                band = jnp.where(here, first, none)
                if before is not None:
                    band = jnp.where(before, second, band)
                bands[block, pl.ds(part * 16, 16), :] = band
                before = here
            for start in range(0, TARGETS, 32):
                part = pl.ds(start, 32)
                d = [towards[a, part, :] - place[a] for a in range(3)]
                inv = lax.rsqrt(d[0] * d[0] + d[1] * d[1] + d[2] * d[2] + 16.0)
                four = 4.0 * inv
                square = four * inv
                greens[block, 0, part, :] = four
                for a in range(3):
                    greens[block, a + 1, part, :] = square * d[a]

    def radiate(group, steps, fresh):
        start = group * n_z
        columns = []
        for j in range(n_z):
            block = start + j
            v = [values[step, block] for step in steps]
            pieces = [[] for _ in steps]
            for begin in range(0, TARGETS, 32):
                green = [greens[block, c, pl.ds(begin, 32), :] for c in range(4)]
                for at in range(len(steps)):
                    term = green[0] * v[at][0:1]
                    for c in range(1, 4):
                        term = term + green[c] * v[at][c : c + 1]
                    pieces[at].append(term.astype(BF16))
            columns.append(jnp.concatenate([piece for step in pieces for piece in step], axis=0))
        rhs = jnp.concatenate(columns, axis=1)
        lhs = jnp.concatenate([bands[start + j] for j in range(n_z)], axis=1)
        span = slice(steps[0] * TARGETS, (steps[-1] + 1) * TARGETS)
        out = lax.dot_general(lhs, rhs, (((1,), (1,)), ((), ())), preferred_element_type=F32)
        if fresh:
            sums[:, span] = out
        else:
            sums[:, span] += out

    def meta_refs():
        return (meta, meta_z_send, meta_z_recv)

    def meta_y_refs():
        return (meta, meta_y_send, meta_y_recv)

    def val_refs(step):
        return (values.at[step], val_z_send.at[step], val_z_recv.at[step])

    def val_y_refs(step):
        return (values.at[step], val_y_send.at[step], val_y_recv.at[step])

    result_copy = pltpu.make_async_copy(last, flow_out, in_sem.at[len(inputs)])
    halos = halo_copies()
    for copy in halos:
        copy.start()
    z_start(*meta_refs())
    onehot[...] = jnp.where(
        lax.broadcasted_iota(jnp.int32, (size_x * size_y, SLOTS), 0) == row_of, 1.0, 0.0
    ).astype(BF16)
    extent = (size_x * n_cfd, size_y * n_obs, size_z)
    for a in range(3):
        line = spots[a : a + 1] * float(extent[a])
        towards[a] = jnp.transpose(jnp.broadcast_to(line, (SLOTS, TARGETS)))
    z_wait(*meta_refs())
    y_start(*meta_y_refs())
    prepare(here_y)
    for copy in halos:
        copy.wait()
    outside(0)
    for step in range(STEPS):
        advance(step)
        if step < STEPS - 1:
            outside(step + 1)
        sample(step)
        z_start(*val_refs(step))
    result_copy.start()
    for far in range(1, n_y):
        y_wait_recv(*meta_y_refs(), far)
        prepare(group_at(far))
    for step in range(STEPS):
        z_wait(*val_refs(step))
        y_start(*val_y_refs(step))
    radiate(here_y, range(STEPS), True)
    for steps in ((0, 1), (2, 3)):
        for far in range(1, n_y):
            for step in steps:
                y_wait_recv(*val_y_refs(step), far)
            radiate(group_at(far), steps, False)

    total = sums[:, :TARGETS]
    for step in range(1, STEPS):
        total = total + pltpu.roll(sums[:, step * TARGETS : (step + 1) * TARGETS], step, 0)
    whole[...] = jnp.transpose(total)

    def part_copy(far):
        return pltpu.make_async_remote_copy(
            src_ref=whole.at[pl.ds(pl.multiple_of(along_obs(far) * owned, owned), owned)],
            dst_ref=parts.at[far - 1],
            send_sem=part_send.at[far - 1],
            recv_sem=part_recv.at[far - 1],
            device_id=(cfd, along_obs(far)),
            device_id_type=MESH,
        )

    for far in range(1, n_obs):
        part_copy(far).start()
    z_wait_send(*meta_refs())
    y_wait_send(*meta_y_refs())
    for step in range(STEPS):
        z_wait_send(*val_refs(step))
        y_wait_send(*val_y_refs(step))
    result_copy.wait()
    result = whole[pl.ds(pl.multiple_of(obs * owned, owned), owned), :]
    for far in range(1, n_obs):
        part_copy(far).wait()
        result = result + parts[far - 1]
    signal[...] = result


def per_device(rings, flow_field, disk_mask, surf_cell, delay_bin, tap_phase, panel_counts, observer_pos):
    n_y, n_z, n_obs = rings
    n_cfd = n_y * n_z
    _, size_x, size_y, size_z = flow_field.shape
    wide = (size_x + 2 * WIDTH, size_y + 2 * SIDE, size_z)
    owned = TARGETS // n_obs
    dma = pltpu.SemaphoreType.DMA
    anywhere = pl.BlockSpec(memory_space=pl.ANY)
    vmem = pl.BlockSpec(memory_space=pltpu.VMEM)
    return pl.pallas_call(
        functools.partial(kernel, rings),
        out_shape=(
            jax.ShapeDtypeStruct(flow_field.shape, F32),
            jax.ShapeDtypeStruct((owned, SAMPLES), F32),
        ),
        in_specs=[anywhere] * 7,
        out_specs=(anywhere, vmem),
        scratch_shapes=[
            pltpu.VMEM(disk_mask.shape, jnp.int32),
            pltpu.VMEM(surf_cell.shape, jnp.int32),
            pltpu.VMEM(delay_bin.shape, jnp.int32),
            pltpu.VMEM(tap_phase.shape, jnp.int32),
            pltpu.VMEM(panel_counts.shape, jnp.int32),
            pltpu.VMEM(observer_pos.shape, F32),
            dma((8,)),
            pltpu.VMEM((5,) + wide, F32),
            pltpu.VMEM((STEPS - 1, 4) + wide, F32),
            pltpu.VMEM(flow_field.shape, F32),
            pltpu.VMEM((n_cfd, 4, SLOTS), F32),
            pltpu.VMEM((STEPS, n_cfd, 4, SLOTS), F32),
            pltpu.VMEM((size_x * size_y, SLOTS), BF16),
            pltpu.VMEM((3, TARGETS, SLOTS), F32),
            pltpu.VMEM((n_cfd, 4, TARGETS, SLOTS), F32),
            pltpu.VMEM((n_cfd, SAMPLES, SLOTS), BF16),
            pltpu.VMEM((SAMPLES, STEPS * TARGETS), F32),
            pltpu.VMEM((TARGETS, SAMPLES), F32),
            pltpu.VMEM((n_obs - 1, owned, SAMPLES), F32),
            dma((8,)),
            dma((8,)),
            dma((n_z,)),
            dma((n_z,)),
            dma((n_y,)),
            dma((n_y,)),
            dma((STEPS, n_z)),
            dma((STEPS, n_z)),
            dma((STEPS, n_y)),
            dma((STEPS, n_y)),
            dma((n_obs - 1,)),
            dma((n_obs - 1,)),
        ],
        compiler_params=pltpu.CompilerParams(
            collective_id=0, has_side_effects=True, vmem_limit_bytes=64 * 1024 * 1024
        ),
    )(flow_field, disk_mask, surf_cell, delay_bin, tap_phase, panel_counts, observer_pos)


def solution(mesh):
    n_cfd, n_obs = mesh.shape["cfd"], mesh.shape["obs"]
    n_y = 4 if n_cfd >= 16 else 2
    rings = (n_y, n_cfd // n_y, n_obs)
    return jax.shard_map(
        functools.partial(per_device, rings),
        mesh=mesh,
        in_specs=(
            P(None, "cfd", "obs", None),
            P("cfd", "obs", None),
            P("obs", "cfd"),
            P("obs", "cfd"),
            P("obs", "cfd"),
            P(),
            P(None, "cfd"),
        ),
        out_specs=(P(None, "cfd", "obs", None), P(("cfd", "obs"), None)),
        check_vma=False,
    )
```

```python
import functools

import jax
import jax.numpy as jnp
from jax import lax
from jax.experimental import pallas as pl
from jax.experimental.pallas import tpu as pltpu
from jax.sharding import PartitionSpec as P

STEPS = 4
SAMPLES = 512
SLOTS = 128
TARGETS = 128
WIDTH = 4
SIDE = 8
MESH = pl.DeviceIdType.MESH
F32 = jnp.float32
BF16 = jnp.bfloat16


def kernel(
    rings,
    flow_in,
    disk_in,
    cells_in,
    delays_in,
    phases_in,
    counts_in,
    spots_in,
    flow_out,
    signal,
    disk,
    cells,
    delays,
    phases,
    counts,
    spots,
    in_sem,
    wide,
    y_send,
    y_recv,
    corner_send,
    corner_recv,
    state,
    last,
    meta,
    values,
    onehot,
    towards,
    greens,
    bands,
    sums,
    whole,
    parts,
    halo_send,
    halo_recv,
    meta_z_send,
    meta_z_recv,
    meta_y_send,
    meta_y_recv,
    val_z_send,
    val_z_recv,
    val_y_send,
    val_y_recv,
    part_send,
    part_recv,
):
    n_y, n_z, n_obs = rings
    n_cfd = n_y * n_z
    cfd = lax.axis_index("cfd")
    obs = lax.axis_index("obs")
    here_y = cfd // n_z
    here_z = cfd % n_z
    size_x, size_y, size_z = flow_in.shape[1:]
    owned = TARGETS // n_obs
    own_x = slice(WIDTH, WIDTH + size_x)
    own_y = slice(SIDE, SIDE + size_y)
    tall = size_y + 2 * SIDE

    def along_z(far):
        return here_y * n_z + lax.rem(here_z + far, n_z)

    def along_y(far):
        return lax.rem(here_y + far, n_y) * n_z + here_z

    def along_obs(far):
        return lax.rem(obs + far, n_obs)

    cfd_next, cfd_prev = lax.rem(cfd + 1, n_cfd), lax.rem(cfd + n_cfd - 1, n_cfd)
    obs_next, obs_prev = along_obs(1), along_obs(n_obs - 1)

    inputs = [
        pltpu.make_async_copy(src, dst, in_sem.at[i])
        for i, (src, dst) in enumerate(
            [
                (disk_in, disk),
                (flow_in, wide.at[0:4, own_x, own_y]),
                (cells_in, cells),
                (delays_in, delays),
                (phases_in, phases),
                (counts_in, counts),
                (spots_in, spots),
            ]
        )
    ]
    for copy in inputs:
        copy.start()

    barrier = pltpu.get_barrier_semaphore()

    def greet(to_cfd, to_obs):
        pl.semaphore_signal(barrier, inc=1, device_id=(to_cfd, to_obs), device_id_type=MESH)

    for to_cfd in (cfd_next, cfd_prev):
        for to_obs in (obs_next, obs_prev, obs):
            greet(to_cfd, to_obs)
    for far in range(1, n_z):
        greet(along_z(far), obs)
    for far in range(1, n_y):
        greet(along_y(far), obs)
    for far in range(1, n_obs):
        greet(cfd, along_obs(far))

    inputs[0].wait()
    for i in range(size_x):
        wide[4, WIDTH + i, own_y] = disk[i].astype(F32)
    for copy in inputs[1:]:
        copy.wait()

    cell = cells[...]
    row_of = cell >> 7
    live_at = (lax.broadcasted_iota(jnp.int32, counts.shape, 0) == obs) & (
        lax.broadcasted_iota(jnp.int32, counts.shape, 1) == cfd
    )
    own = jnp.sum(jnp.where(live_at, counts[...], 0).astype(F32), axis=(0, 1), keepdims=True)
    live = lax.broadcasted_iota(jnp.int32, (1, SLOTS), 1).astype(F32) < own
    meta[cfd] = jnp.concatenate(
        [
            cell.astype(F32),
            delays[...].astype(F32),
            phases[...].astype(F32),
            jnp.zeros((1, SLOTS), F32),
        ],
        axis=0,
    )

    last_x, last_y = WIDTH + size_x - 1, SIDE + size_y - 1
    corners = [
        (x_side, y_side)
        for x_side in ((cfd_next, last_x, -1, WIDTH - 1), (cfd_prev, WIDTH, 1, last_x + 1))
        for y_side in ((obs_next, True), (obs_prev, False))
    ]

    def pack():
        y_send[0] = wide[:, own_x, last_y - WIDTH + 1 : last_y + 1]
        y_send[1] = wide[:, own_x, SIDE : SIDE + WIDTH]
        for at, ((_, x, turn, _), (_, upper)) in enumerate(corners):
            for c in range(5):
                pieces = []
                for far in range(1, WIDTH):
                    many = WIDTH - far
                    rows = slice(last_y + 1 - many, last_y + 1) if upper else slice(SIDE, SIDE + many)
                    pieces.append(wide[c, x + turn * (far - 1), rows])
                corner_send[at, c] = jnp.concatenate(pieces + [jnp.zeros((2, size_z), F32)], axis=0)

    def unpack():
        wide[:, own_x, SIDE - WIDTH : SIDE] = y_recv[0]
        wide[:, own_x, last_y + 1 : last_y + 1 + WIDTH] = y_recv[1]
        for at, ((_, _, turn, x), (_, upper)) in enumerate(corners):
            for c in range(5):
                begin = 0
                for far in range(1, WIDTH):
                    many = WIDTH - far
                    rows = slice(SIDE - many, SIDE) if upper else slice(last_y + 1, last_y + 1 + many)
                    wide[c, x + turn * (far - 1), rows] = corner_recv[at, c, begin : begin + many]
                    begin += many

    def halo_copies():
        moves = [
            (wide.at[:, size_x : size_x + WIDTH, own_y], wide.at[:, 0:WIDTH, own_y], cfd_next, obs),
            (
                wide.at[:, WIDTH : 2 * WIDTH, own_y],
                wide.at[:, WIDTH + size_x : 2 * WIDTH + size_x, own_y],
                cfd_prev,
                obs,
            ),
            (y_send.at[0], y_recv.at[0], cfd, obs_next),
            (y_send.at[1], y_recv.at[1], cfd, obs_prev),
        ]
        for at, ((to_cfd, _, _, _), (to_obs, _)) in enumerate(corners):
            moves.append((corner_send.at[at], corner_recv.at[at], to_cfd, to_obs))
        return [
            pltpu.make_async_remote_copy(
                src_ref=source,
                dst_ref=target,
                send_sem=halo_send.at[i],
                recv_sem=halo_recv.at[i],
                device_id=(to_cfd, to_obs),
                device_id_type=MESH,
            )
            for i, (source, target, to_cfd, to_obs) in enumerate(moves)
        ]

    def fields(step):
        return wide if step == 0 else state.at[step - 1]

    def outside(step):
        ref = fields(step)

        @pl.when(cfd == 0)
        def _():
            ref[0:4, 0:WIDTH] = jnp.zeros((4, WIDTH, tall, size_z), F32)

        @pl.when(cfd == n_cfd - 1)
        def _():
            ref[0:4, WIDTH + size_x :] = jnp.zeros((4, WIDTH, tall, size_z), F32)

        @pl.when(obs == 0)
        def _():
            ref[0:4, :, 0:SIDE] = jnp.zeros((4, size_x + 2 * WIDTH, SIDE, size_z), F32)

        @pl.when(obs == n_obs - 1)
        def _():
            ref[0:4, :, SIDE + size_y :] = jnp.zeros((4, size_x + 2 * WIDTH, SIDE, size_z), F32)

    lane = lax.broadcasted_iota(jnp.int32, (tall, size_z), 1)

    def advance(step):
        ref = fields(step)
        final = step == STEPS - 1

        @pl.loop(1 + step, 2 * WIDTH + size_x - 1 - step, unroll=True)
        def _(i):
            slabs = [ref[c, i] for c in range(4)]
            there = wide[4, i]
            for c in range(4):
                q = slabs[c]
                near = (
                    q
                    + ref[c, i + 1]
                    + pltpu.roll(q, 1, 0)
                    + pltpu.roll(q, tall - 1, 0)
                    + jnp.where(lane == 0, 0.0, pltpu.roll(q, 1, 1))
                    + jnp.where(lane == size_z - 1, 0.0, pltpu.roll(q, size_z - 1, 1))
                )
                pull = 0.5 * slabs[1] if c == 0 else -0.4 * q
                moved = 0.1 * near + 0.4 * ref[c, i - 1] + there * pull
                if final:
                    last[c, i - WIDTH] = moved[own_y]
                else:
                    state[step, c, i] = moved

    def sample(step):
        for c in range(4):
            block = last[c] if step == STEPS - 1 else state[step, c, own_x, own_y]
            q = block.reshape(size_x * size_y, size_z)
            high = q.astype(BF16)
            low = (q - high.astype(F32)).astype(BF16)
            dims = (((0,), (0,)), ((), ()))
            lines = lax.dot_general(high, onehot[...], dims, preferred_element_type=F32)
            lines = lines + lax.dot_general(low, onehot[...], dims, preferred_element_type=F32)
            z_at = lax.broadcasted_iota(jnp.int32, (size_z, SLOTS), 0) == (cells[...] & 127)
            v = jnp.sum(jnp.where(z_at, lines, 0.0), axis=0, keepdims=True)
            values[step, cfd, c : c + 1, :] = jnp.where(live, v, 0.0)

    def z_copy(buf, block, send, recv, far, source):
        return pltpu.make_async_remote_copy(
            src_ref=buf.at[block],
            dst_ref=buf.at[block],
            send_sem=send.at[far],
            recv_sem=recv.at[source],
            device_id=(along_z(far), obs),
            device_id_type=MESH,
        )

    def z_start(buf, send, recv):
        @pl.loop(0, n_z - 1)
        def _(k):
            far = 1 + lax.rem(k + n_z // 2 - 1, n_z - 1)
            z_copy(buf, cfd, send, recv, far, far).start()

    def z_wait(buf, send, recv):
        @pl.loop(1, n_z)
        def _(far):
            source = here_y * n_z + lax.rem(here_z + n_z - far, n_z)
            z_copy(buf, source, send, recv, far, far).wait_recv()

    def z_wait_send(buf, send, recv):
        @pl.loop(1, n_z)
        def _(far):
            z_copy(buf, cfd, send, recv, far, far).wait_send()

    def y_group(buf, group, send, recv, far):
        block = pl.ds(pl.multiple_of(group * n_z, n_z), n_z)
        return pltpu.make_async_remote_copy(
            src_ref=buf.at[block],
            dst_ref=buf.at[block],
            send_sem=send.at[far],
            recv_sem=recv.at[far],
            device_id=(along_y(far), obs),
            device_id_type=MESH,
        )

    def group_at(back):
        return lax.rem(here_y + n_y - back, n_y)

    def y_start(buf, send, recv):
        for far in range(1, n_y):
            y_group(buf, here_y, send, recv, far).start()

    def y_wait_recv(buf, send, recv, far):
        y_group(buf, group_at(far), send, recv, far).wait_recv()

    def y_wait_send(buf, send, recv):
        for far in range(1, n_y):
            y_group(buf, here_y, send, recv, far).wait_send()

    def prepare(group):
        at = lax.broadcasted_iota(jnp.int32, (16, SLOTS), 0).astype(F32)
        none = jnp.zeros((16, SLOTS), BF16)

        @pl.loop(0, n_z, unroll=4)
        def _(k):
            block = group * n_z + k
            rows = meta[block]
            where = rows[0:1]
            slab = jnp.floor(where * (1.0 / (size_y * size_z)))
            inner = where - float(size_y * size_z) * slab
            line = jnp.floor(inner * (1.0 / size_z))
            place = [
                slab + ((block * size_x).astype(F32) + 0.5),
                line + ((obs * size_y).astype(F32) + 0.5),
                inner - float(size_z) * line + 0.5,
            ]
            delay = rows[1:2]
            frac = rows[2:3] * 0.25
            weights = [
                -frac * (frac - 1.0) * (frac - 2.0) / 6.0,
                (frac + 1.0) * (frac - 1.0) * (frac - 2.0) * 0.5,
                -(frac + 1.0) * frac * (frac - 2.0) * 0.5,
                (frac + 1.0) * frac * (frac - 1.0) / 6.0,
            ]
            high = jnp.floor(delay * 0.0625)
            low = delay - 16.0 * high
            first, second = jnp.zeros((16, SLOTS), F32), jnp.zeros((16, SLOTS), F32)
            for tap in range(4):
                first = jnp.where(at == low + float(tap), weights[tap], first)
                second = jnp.where(at + 16.0 == low + float(tap), weights[tap], second)
            first, second = first.astype(BF16), second.astype(BF16)
            high = jnp.broadcast_to(high, (16, SLOTS)).astype(BF16)
            before = None
            for part in range(SAMPLES // 16):
                here = high == jnp.asarray(float(part), BF16)
                band = jnp.where(here, first, none)
                if before is not None:
                    band = jnp.where(before, second, band)
                bands[block, pl.ds(part * 16, 16), :] = band
                before = here
            for start in range(0, TARGETS, 32):
                part = pl.ds(start, 32)
                d = [towards[a, part, :] - place[a] for a in range(3)]
                inv = lax.rsqrt(d[0] * d[0] + d[1] * d[1] + d[2] * d[2] + 16.0)
                four = 4.0 * inv
                square = four * inv
                greens[block, 0, part, :] = four
                for a in range(3):
                    greens[block, a + 1, part, :] = square * d[a]

    def radiate(group, steps):
        start = group * n_z
        columns = []
        for j in range(n_z):
            block = start + j
            v = [values[step, block] for step in steps]
            pieces = [[] for _ in steps]
            for begin in range(0, TARGETS, 32):
                green = [greens[block, c, pl.ds(begin, 32), :] for c in range(4)]
                for at in range(len(steps)):
                    term = green[0] * v[at][0:1]
                    for c in range(1, 4):
                        term = term + green[c] * v[at][c : c + 1]
                    pieces[at].append(term.astype(BF16))
            columns.append(jnp.concatenate([piece for step in pieces for piece in step], axis=0))
        rhs = jnp.concatenate(columns, axis=1)
        lhs = jnp.concatenate([bands[start + j] for j in range(n_z)], axis=1)
        span = slice(steps[0] * TARGETS, (steps[-1] + 1) * TARGETS)
        out = lax.dot_general(lhs, rhs, (((1,), (1,)), ((), ())), preferred_element_type=F32)
        sums[:, span] += out

    def meta_refs():
        return (meta, meta_z_send, meta_z_recv)

    def meta_y_refs():
        return (meta, meta_y_send, meta_y_recv)

    def val_refs(step):
        return (values.at[step], val_z_send.at[step], val_z_recv.at[step])

    def val_y_refs(step):
        return (values.at[step], val_y_send.at[step], val_y_recv.at[step])

    pack()
    pl.semaphore_wait(barrier, 6 + n_z - 1 + n_y - 1 + n_obs - 1)
    result_copy = pltpu.make_async_copy(last, flow_out, in_sem.at[len(inputs)])
    halos = halo_copies()
    for copy in halos:
        copy.start()
    z_start(*meta_refs())
    onehot[...] = jnp.where(
        lax.broadcasted_iota(jnp.int32, (size_x * size_y, SLOTS), 0) == row_of, 1.0, 0.0
    ).astype(BF16)
    extent = (size_x * n_cfd, size_y * n_obs, size_z)
    for a in range(3):
        line = spots[a : a + 1] * float(extent[a])
        towards[a] = jnp.transpose(jnp.broadcast_to(line, (SLOTS, TARGETS)))
    for copy in halos:
        copy.wait()
    unpack()
    outside(0)
    for step in range(STEPS):
        advance(step)
        if step < STEPS - 1:
            outside(step + 1)
        sample(step)
        z_start(*val_refs(step))
        if step == 0:
            z_wait(*meta_refs())
            y_start(*meta_y_refs())
    result_copy.start()
    prepare(here_y)

    @pl.loop(1, n_y)
    def _(far):
        y_wait_recv(*meta_y_refs(), far)
        prepare(group_at(far))

    for step in range(STEPS):
        z_wait(*val_refs(step))
        y_start(*val_y_refs(step))
    sums[...] = jnp.zeros_like(sums)
    radiate(here_y, range(STEPS))
    for steps in ((0, 1), (2, 3)):

        @pl.loop(1, n_y)
        def _(far):
            for step in steps:
                y_wait_recv(*val_y_refs(step), far)
            radiate(group_at(far), steps)

    total = sums[:, :TARGETS]
    for step in range(1, STEPS):
        total = total + pltpu.roll(sums[:, step * TARGETS : (step + 1) * TARGETS], step, 0)
    whole[...] = jnp.transpose(total)

    def part_copy(far):
        return pltpu.make_async_remote_copy(
            src_ref=whole.at[pl.ds(pl.multiple_of(along_obs(far) * owned, owned), owned)],
            dst_ref=parts.at[far - 1],
            send_sem=part_send.at[far - 1],
            recv_sem=part_recv.at[far - 1],
            device_id=(cfd, along_obs(far)),
            device_id_type=MESH,
        )

    for far in range(1, n_obs):
        part_copy(far).start()
    z_wait_send(*meta_refs())
    y_wait_send(*meta_y_refs())
    for step in range(STEPS):
        z_wait_send(*val_refs(step))
        y_wait_send(*val_y_refs(step))
    result_copy.wait()
    result = whole[pl.ds(pl.multiple_of(obs * owned, owned), owned), :]
    for far in range(1, n_obs):
        part_copy(far).wait()
        result = result + parts[far - 1]
    signal[...] = result


def per_device(rings, flow_field, disk_mask, surf_cell, delay_bin, tap_phase, panel_counts, observer_pos):
    n_y, n_z, n_obs = rings
    n_cfd = n_y * n_z
    _, size_x, size_y, size_z = flow_field.shape
    wide = (size_x + 2 * WIDTH, size_y + 2 * SIDE, size_z)
    owned = TARGETS // n_obs
    dma = pltpu.SemaphoreType.DMA
    anywhere = pl.BlockSpec(memory_space=pl.ANY)
    vmem = pl.BlockSpec(memory_space=pltpu.VMEM)
    return pl.pallas_call(
        functools.partial(kernel, rings),
        out_shape=(
            jax.ShapeDtypeStruct(flow_field.shape, F32),
            jax.ShapeDtypeStruct((owned, SAMPLES), F32),
        ),
        in_specs=[anywhere] * 7,
        out_specs=(anywhere, vmem),
        scratch_shapes=[
            pltpu.VMEM(disk_mask.shape, jnp.int32),
            pltpu.VMEM(surf_cell.shape, jnp.int32),
            pltpu.VMEM(delay_bin.shape, jnp.int32),
            pltpu.VMEM(tap_phase.shape, jnp.int32),
            pltpu.VMEM(panel_counts.shape, jnp.int32),
            pltpu.VMEM(observer_pos.shape, F32),
            dma((8,)),
            pltpu.VMEM((5,) + wide, F32),
            pltpu.VMEM((2, 5, size_x, WIDTH, size_z), F32),
            pltpu.VMEM((2, 5, size_x, WIDTH, size_z), F32),
            pltpu.VMEM((4, 5, 8, size_z), F32),
            pltpu.VMEM((4, 5, 8, size_z), F32),
            pltpu.VMEM((STEPS - 1, 4) + wide, F32),
            pltpu.VMEM(flow_field.shape, F32),
            pltpu.VMEM((n_cfd, 4, SLOTS), F32),
            pltpu.VMEM((STEPS, n_cfd, 4, SLOTS), F32),
            pltpu.VMEM((size_x * size_y, SLOTS), BF16),
            pltpu.VMEM((3, TARGETS, SLOTS), F32),
            pltpu.VMEM((n_cfd, 4, TARGETS, SLOTS), F32),
            pltpu.VMEM((n_cfd, SAMPLES, SLOTS), BF16),
            pltpu.VMEM((SAMPLES, STEPS * TARGETS), F32),
            pltpu.VMEM((TARGETS, SAMPLES), F32),
            pltpu.VMEM((n_obs - 1, owned, SAMPLES), F32),
            dma((8,)),
            dma((8,)),
            dma((n_z,)),
            dma((n_z,)),
            dma((n_y,)),
            dma((n_y,)),
            dma((STEPS, n_z)),
            dma((STEPS, n_z)),
            dma((STEPS, n_y)),
            dma((STEPS, n_y)),
            dma((n_obs - 1,)),
            dma((n_obs - 1,)),
        ],
        compiler_params=pltpu.CompilerParams(
            collective_id=0, has_side_effects=True, vmem_limit_bytes=64 * 1024 * 1024
        ),
    )(flow_field, disk_mask, surf_cell, delay_bin, tap_phase, panel_counts, observer_pos)


def solution(mesh):
    n_cfd, n_obs = mesh.shape["cfd"], mesh.shape["obs"]
    n_y = 4 if n_cfd >= 16 else 2
    rings = (n_y, n_cfd // n_y, n_obs)
    return jax.shard_map(
        functools.partial(per_device, rings),
        mesh=mesh,
        in_specs=(
            P(None, "cfd", "obs", None),
            P("cfd", "obs", None),
            P("obs", "cfd"),
            P("obs", "cfd"),
            P("obs", "cfd"),
            P(),
            P(None, "cfd"),
        ),
        out_specs=(P(None, "cfd", "obs", None), P(("cfd", "obs"), None)),
        check_vma=False,
    )
```

```python
import functools

import jax
import jax.numpy as jnp
from jax import lax
from jax.experimental import pallas as pl
from jax.experimental.pallas import tpu as pltpu
from jax.sharding import PartitionSpec as P

STEPS = 4
SAMPLES = 512
SLOTS = 128
TARGETS = 128
WIDTH = 4
SIDE = 8
MESH = pl.DeviceIdType.MESH
F32 = jnp.float32
BF16 = jnp.bfloat16


def kernel(
    rings,
    flow_in,
    disk_in,
    cells_in,
    delays_in,
    phases_in,
    counts_in,
    spots_in,
    flow_out,
    signal,
    disk,
    cells,
    delays,
    phases,
    counts,
    spots,
    in_sem,
    wide,
    y_send,
    y_recv,
    corner_send,
    corner_recv,
    state,
    last,
    meta,
    values,
    onehot,
    towards,
    greens,
    bands,
    sums,
    whole,
    parts,
    halo_send,
    halo_recv,
    meta_z_send,
    meta_z_recv,
    meta_y_send,
    meta_y_recv,
    val_z_send,
    val_z_recv,
    val_y_send,
    val_y_recv,
    part_send,
    part_recv,
):
    n_y, n_z, n_obs = rings
    n_cfd = n_y * n_z
    cfd = lax.axis_index("cfd")
    obs = lax.axis_index("obs")
    here_y = cfd // n_z
    here_z = cfd % n_z
    size_x, size_y, size_z = flow_in.shape[1:]
    owned = TARGETS // n_obs
    own_x = slice(WIDTH, WIDTH + size_x)
    own_y = slice(SIDE, SIDE + size_y)
    tall = size_y + 2 * SIDE

    def along_z(far):
        return here_y * n_z + lax.rem(here_z + far, n_z)

    def along_y(far):
        return lax.rem(here_y + far, n_y) * n_z + here_z

    def along_obs(far):
        return lax.rem(obs + far, n_obs)

    cfd_next, cfd_prev = lax.rem(cfd + 1, n_cfd), lax.rem(cfd + n_cfd - 1, n_cfd)
    obs_next, obs_prev = along_obs(1), along_obs(n_obs - 1)

    inputs = [
        pltpu.make_async_copy(src, dst, in_sem.at[i])
        for i, (src, dst) in enumerate(
            [
                (disk_in, disk),
                (flow_in, wide.at[0:4, own_x, own_y]),
                (cells_in, cells),
                (delays_in, delays),
                (phases_in, phases),
                (counts_in, counts),
                (spots_in, spots),
            ]
        )
    ]
    for copy in inputs:
        copy.start()

    barrier = pltpu.get_barrier_semaphore()

    def greet(to_cfd, to_obs):
        pl.semaphore_signal(barrier, inc=1, device_id=(to_cfd, to_obs), device_id_type=MESH)

    for to_cfd in (cfd_next, cfd_prev):
        for to_obs in (obs_next, obs_prev, obs):
            greet(to_cfd, to_obs)
    for far in range(1, n_z):
        greet(along_z(far), obs)
    for far in range(1, n_y):
        greet(along_y(far), obs)
    for far in range(1, n_obs):
        greet(cfd, along_obs(far))

    inputs[0].wait()
    for i in range(size_x):
        wide[4, WIDTH + i, own_y] = disk[i].astype(F32)
    for copy in inputs[1:]:
        copy.wait()

    cell = cells[...]
    row_of = cell >> 7
    live_at = (lax.broadcasted_iota(jnp.int32, counts.shape, 0) == obs) & (
        lax.broadcasted_iota(jnp.int32, counts.shape, 1) == cfd
    )
    own = jnp.sum(jnp.where(live_at, counts[...], 0).astype(F32), axis=(0, 1), keepdims=True)
    live = lax.broadcasted_iota(jnp.int32, (1, SLOTS), 1).astype(F32) < own
    meta[cfd] = jnp.concatenate(
        [
            cell.astype(F32),
            delays[...].astype(F32),
            phases[...].astype(F32),
            jnp.zeros((1, SLOTS), F32),
        ],
        axis=0,
    )

    last_x, last_y = WIDTH + size_x - 1, SIDE + size_y - 1
    corners = [
        (x_side, y_side)
        for x_side in ((cfd_next, last_x, -1, WIDTH - 1), (cfd_prev, WIDTH, 1, last_x + 1))
        for y_side in ((obs_next, True), (obs_prev, False))
    ]

    def pack():
        y_send[0] = wide[:, own_x, last_y - WIDTH + 1 : last_y + 1]
        y_send[1] = wide[:, own_x, SIDE : SIDE + WIDTH]
        for at, ((_, x, turn, _), (_, upper)) in enumerate(corners):
            for c in range(5):
                pieces = []
                for far in range(1, WIDTH):
                    many = WIDTH - far
                    rows = slice(last_y + 1 - many, last_y + 1) if upper else slice(SIDE, SIDE + many)
                    pieces.append(wide[c, x + turn * (far - 1), rows])
                corner_send[at, c] = jnp.concatenate(pieces + [jnp.zeros((2, size_z), F32)], axis=0)

    def unpack_y():
        wide[:, own_x, SIDE - WIDTH : SIDE] = y_recv[0]
        wide[:, own_x, last_y + 1 : last_y + 1 + WIDTH] = y_recv[1]

    def unpack_corners():
        for at, ((_, _, turn, x), (_, upper)) in enumerate(corners):
            for c in range(5):
                begin = 0
                for far in range(1, WIDTH):
                    many = WIDTH - far
                    rows = slice(SIDE - many, SIDE) if upper else slice(last_y + 1, last_y + 1 + many)
                    wide[c, x + turn * (far - 1), rows] = corner_recv[at, c, begin : begin + many]
                    begin += many

    def halo_copies():
        moves = [
            (y_send.at[0], y_recv.at[0], cfd, obs_next),
            (y_send.at[1], y_recv.at[1], cfd, obs_prev),
            (wide.at[:, size_x : size_x + WIDTH, own_y], wide.at[:, 0:WIDTH, own_y], cfd_next, obs),
            (
                wide.at[:, WIDTH : 2 * WIDTH, own_y],
                wide.at[:, WIDTH + size_x : 2 * WIDTH + size_x, own_y],
                cfd_prev,
                obs,
            ),
        ]
        for at, ((to_cfd, _, _, _), (to_obs, _)) in enumerate(corners):
            moves.append((corner_send.at[at], corner_recv.at[at], to_cfd, to_obs))
        return [
            pltpu.make_async_remote_copy(
                src_ref=source,
                dst_ref=target,
                send_sem=halo_send.at[i],
                recv_sem=halo_recv.at[i],
                device_id=(to_cfd, to_obs),
                device_id_type=MESH,
            )
            for i, (source, target, to_cfd, to_obs) in enumerate(moves)
        ]

    def fields(step):
        return wide if step == 0 else state.at[step - 1]

    def outside_x(step):
        ref = fields(step)

        @pl.when(cfd == 0)
        def _():
            ref[0:4, 0:WIDTH] = jnp.zeros((4, WIDTH, tall, size_z), F32)

        @pl.when(cfd == n_cfd - 1)
        def _():
            ref[0:4, WIDTH + size_x :] = jnp.zeros((4, WIDTH, tall, size_z), F32)

    def outside_y(step):
        ref = fields(step)

        @pl.when(obs == 0)
        def _():
            ref[0:4, :, 0:SIDE] = jnp.zeros((4, size_x + 2 * WIDTH, SIDE, size_z), F32)

        @pl.when(obs == n_obs - 1)
        def _():
            ref[0:4, :, SIDE + size_y :] = jnp.zeros((4, size_x + 2 * WIDTH, SIDE, size_z), F32)

    lane = lax.broadcasted_iota(jnp.int32, (tall, size_z), 1)

    def advance(step, begin, end):
        ref = fields(step)
        final = step == STEPS - 1

        @pl.loop(begin, end, unroll=True)
        def _(i):
            slabs = [ref[c, i] for c in range(4)]
            there = wide[4, i]
            for c in range(4):
                q = slabs[c]
                near = (
                    q
                    + ref[c, i + 1]
                    + pltpu.roll(q, 1, 0)
                    + pltpu.roll(q, tall - 1, 0)
                    + jnp.where(lane == 0, 0.0, pltpu.roll(q, 1, 1))
                    + jnp.where(lane == size_z - 1, 0.0, pltpu.roll(q, size_z - 1, 1))
                )
                pull = 0.5 * slabs[1] if c == 0 else -0.4 * q
                moved = 0.1 * near + 0.4 * ref[c, i - 1] + there * pull
                if final:
                    last[c, i - WIDTH] = moved[own_y]
                else:
                    state[step, c, i] = moved

    def sample(step):
        for c in range(4):
            block = last[c] if step == STEPS - 1 else state[step, c, own_x, own_y]
            q = block.reshape(size_x * size_y, size_z)
            high = q.astype(BF16)
            low = (q - high.astype(F32)).astype(BF16)
            dims = (((0,), (0,)), ((), ()))
            lines = lax.dot_general(high, onehot[...], dims, preferred_element_type=F32)
            lines = lines + lax.dot_general(low, onehot[...], dims, preferred_element_type=F32)
            z_at = lax.broadcasted_iota(jnp.int32, (size_z, SLOTS), 0) == (cells[...] & 127)
            v = jnp.sum(jnp.where(z_at, lines, 0.0), axis=0, keepdims=True)
            at = step % 2 * 4 + c
            values[step // 2, cfd, at : at + 1, :] = jnp.where(live, v, 0.0)

    def z_copy(buf, block, send, recv, far, source):
        return pltpu.make_async_remote_copy(
            src_ref=buf.at[block],
            dst_ref=buf.at[block],
            send_sem=send.at[far],
            recv_sem=recv.at[source],
            device_id=(along_z(far), obs),
            device_id_type=MESH,
        )

    def z_start(buf, send, recv):
        @pl.loop(0, n_z - 1)
        def _(k):
            far = n_z // 2 + (1 - 2 * (k % 2)) * ((k + 1) // 2)
            z_copy(buf, cfd, send, recv, far, far).start()

    def z_wait(buf, send, recv):
        @pl.loop(1, n_z)
        def _(far):
            source = here_y * n_z + lax.rem(here_z + n_z - far, n_z)
            z_copy(buf, source, send, recv, far, far).wait_recv()

    def z_wait_send(buf, send, recv):
        @pl.loop(1, n_z)
        def _(far):
            z_copy(buf, cfd, send, recv, far, far).wait_send()

    def y_group(buf, group, send, recv, far):
        block = pl.ds(pl.multiple_of(group * n_z, n_z), n_z)
        return pltpu.make_async_remote_copy(
            src_ref=buf.at[block],
            dst_ref=buf.at[block],
            send_sem=send.at[far],
            recv_sem=recv.at[far],
            device_id=(along_y(far), obs),
            device_id_type=MESH,
        )

    def group_at(back):
        return lax.rem(here_y + n_y - back, n_y)

    def y_start(buf, send, recv):
        for far in range(1, n_y):
            y_group(buf, here_y, send, recv, far).start()

    def y_wait_recv(buf, send, recv, far):
        y_group(buf, group_at(far), send, recv, far).wait_recv()

    def y_wait_send(buf, send, recv):
        for far in range(1, n_y):
            y_group(buf, here_y, send, recv, far).wait_send()

    def prepare(group):
        at = lax.broadcasted_iota(jnp.int32, (16, SLOTS), 0).astype(F32)
        none = jnp.zeros((16, SLOTS), BF16)

        @pl.loop(0, n_z, unroll=4)
        def _(k):
            block = group * n_z + k
            rows = meta[block]
            where = rows[0:1]
            slab = jnp.floor(where * (1.0 / (size_y * size_z)))
            inner = where - float(size_y * size_z) * slab
            line = jnp.floor(inner * (1.0 / size_z))
            place = [
                slab + ((block * size_x).astype(F32) + 0.5),
                line + ((obs * size_y).astype(F32) + 0.5),
                inner - float(size_z) * line + 0.5,
            ]
            delay = rows[1:2]
            frac = rows[2:3] * 0.25
            weights = [
                -frac * (frac - 1.0) * (frac - 2.0) / 6.0,
                (frac + 1.0) * (frac - 1.0) * (frac - 2.0) * 0.5,
                -(frac + 1.0) * frac * (frac - 2.0) * 0.5,
                (frac + 1.0) * frac * (frac - 1.0) / 6.0,
            ]
            high = jnp.floor(delay * 0.0625)
            low = delay - 16.0 * high
            first, second = jnp.zeros((16, SLOTS), F32), jnp.zeros((16, SLOTS), F32)
            for tap in range(4):
                first = jnp.where(at == low + float(tap), weights[tap], first)
                second = jnp.where(at + 16.0 == low + float(tap), weights[tap], second)
            first, second = first.astype(BF16), second.astype(BF16)
            high = jnp.broadcast_to(high, (16, SLOTS)).astype(BF16)
            before = None
            for part in range(SAMPLES // 16):
                here = high == jnp.asarray(float(part), BF16)
                band = jnp.where(here, first, none)
                if before is not None:
                    band = jnp.where(before, second, band)
                bands[block, pl.ds(part * 16, 16), :] = band
                before = here
            for start in range(0, TARGETS, 32):
                part = pl.ds(start, 32)
                d = [towards[a, part, :] - place[a] for a in range(3)]
                inv = lax.rsqrt(d[0] * d[0] + d[1] * d[1] + d[2] * d[2] + 16.0)
                four = 4.0 * inv
                square = four * inv
                greens[block, 0, part, :] = four
                for a in range(3):
                    greens[block, a + 1, part, :] = square * d[a]

    def radiate(group, steps):
        start = group * n_z
        columns = []
        for j in range(n_z):
            block = start + j
            v = [values[step // 2, block, step % 2 * 4 : step % 2 * 4 + 4] for step in steps]
            pieces = [[] for _ in steps]
            for begin in range(0, TARGETS, 32):
                green = [greens[block, c, pl.ds(begin, 32), :] for c in range(4)]
                for at in range(len(steps)):
                    term = green[0] * v[at][0:1]
                    for c in range(1, 4):
                        term = term + green[c] * v[at][c : c + 1]
                    pieces[at].append(term.astype(BF16))
            columns.append(jnp.concatenate([piece for step in pieces for piece in step], axis=0))
        rhs = jnp.concatenate(columns, axis=1)
        lhs = jnp.concatenate([bands[start + j] for j in range(n_z)], axis=1)
        span = slice(steps[0] * TARGETS, (steps[-1] + 1) * TARGETS)
        out = lax.dot_general(lhs, rhs, (((1,), (1,)), ((), ())), preferred_element_type=F32)
        sums[:, span] += out

    def meta_refs():
        return (meta, meta_z_send, meta_z_recv)

    def meta_y_refs():
        return (meta, meta_y_send, meta_y_recv)

    def val_refs(half):
        return (values.at[half], val_z_send.at[half], val_z_recv.at[half])

    def val_y_refs(half):
        return (values.at[half], val_y_send.at[half], val_y_recv.at[half])

    pack()
    pl.semaphore_wait(barrier, 6 + n_z - 1 + n_y - 1 + n_obs - 1)
    result_copy = pltpu.make_async_copy(last, flow_out, in_sem.at[len(inputs)])
    halos = halo_copies()
    for copy in halos:
        copy.start()
    z_start(*meta_refs())
    onehot[...] = jnp.where(
        lax.broadcasted_iota(jnp.int32, (size_x * size_y, SLOTS), 0) == row_of, 1.0, 0.0
    ).astype(BF16)
    extent = (size_x * n_cfd, size_y * n_obs, size_z)
    for a in range(3):
        line = spots[a : a + 1] * float(extent[a])
        towards[a] = jnp.transpose(jnp.broadcast_to(line, (SLOTS, TARGETS)))
    for copy in halos[:2]:
        copy.wait()
    unpack_y()
    outside_y(0)
    for step in range(STEPS):
        advance(step, WIDTH + 1 + step, WIDTH + size_x - 1 - step)
        if step < STEPS - 1:
            outside_y(step + 1)
    for copy in halos[2:]:
        copy.wait()
    unpack_corners()
    outside_x(0)
    outside_y(0)
    for step in range(STEPS):
        advance(step, 1 + step, WIDTH + 1 + step)
        advance(step, WIDTH + size_x - 1 - step, 2 * WIDTH + size_x - 1 - step)
        if step < STEPS - 1:
            outside_x(step + 1)
            outside_y(step + 1)
        if step % 2 == 1:
            sample(step - 1)
            sample(step)
            z_start(*val_refs(step // 2))
        if step == 1:
            z_wait(*meta_refs())
            y_start(*meta_y_refs())
    result_copy.start()
    prepare(here_y)

    def arrival(k):
        return 1 + 2 * (k - 1) % (n_y - 1)

    @pl.loop(1, n_y)
    def _(k):
        far = arrival(k)
        y_wait_recv(*meta_y_refs(), far)
        prepare(group_at(far))

    for half in range(2):
        z_wait(*val_refs(half))
        y_start(*val_y_refs(half))
    sums[...] = jnp.zeros_like(sums)
    radiate(here_y, range(STEPS))
    for half in range(2):

        @pl.loop(1, n_y)
        def _(k):
            far = arrival(k)
            y_wait_recv(*val_y_refs(half), far)
            radiate(group_at(far), (2 * half, 2 * half + 1))

    total = sums[:, :TARGETS]
    for step in range(1, STEPS):
        total = total + pltpu.roll(sums[:, step * TARGETS : (step + 1) * TARGETS], step, 0)
    whole[...] = jnp.transpose(total)

    def part_copy(far):
        return pltpu.make_async_remote_copy(
            src_ref=whole.at[pl.ds(pl.multiple_of(along_obs(far) * owned, owned), owned)],
            dst_ref=parts.at[far - 1],
            send_sem=part_send.at[far - 1],
            recv_sem=part_recv.at[far - 1],
            device_id=(cfd, along_obs(far)),
            device_id_type=MESH,
        )

    for far in sorted(range(1, n_obs), key=lambda far: abs(far - n_obs // 2)):
        part_copy(far).start()
    z_wait_send(*meta_refs())
    y_wait_send(*meta_y_refs())
    for half in range(2):
        z_wait_send(*val_refs(half))
        y_wait_send(*val_y_refs(half))
    result_copy.wait()
    result = whole[pl.ds(pl.multiple_of(obs * owned, owned), owned), :]
    for far in range(1, n_obs):
        part_copy(far).wait()
        result = result + parts[far - 1]
    signal[...] = result


def per_device(rings, flow_field, disk_mask, surf_cell, delay_bin, tap_phase, panel_counts, observer_pos):
    n_y, n_z, n_obs = rings
    n_cfd = n_y * n_z
    _, size_x, size_y, size_z = flow_field.shape
    wide = (size_x + 2 * WIDTH, size_y + 2 * SIDE, size_z)
    owned = TARGETS // n_obs
    dma = pltpu.SemaphoreType.DMA
    anywhere = pl.BlockSpec(memory_space=pl.ANY)
    vmem = pl.BlockSpec(memory_space=pltpu.VMEM)
    return pl.pallas_call(
        functools.partial(kernel, rings),
        out_shape=(
            jax.ShapeDtypeStruct(flow_field.shape, F32),
            jax.ShapeDtypeStruct((owned, SAMPLES), F32),
        ),
        in_specs=[anywhere] * 7,
        out_specs=(anywhere, vmem),
        scratch_shapes=[
            pltpu.VMEM(disk_mask.shape, jnp.int32),
            pltpu.VMEM(surf_cell.shape, jnp.int32),
            pltpu.VMEM(delay_bin.shape, jnp.int32),
            pltpu.VMEM(tap_phase.shape, jnp.int32),
            pltpu.VMEM(panel_counts.shape, jnp.int32),
            pltpu.VMEM(observer_pos.shape, F32),
            dma((8,)),
            pltpu.VMEM((5,) + wide, F32),
            pltpu.VMEM((2, 5, size_x, WIDTH, size_z), F32),
            pltpu.VMEM((2, 5, size_x, WIDTH, size_z), F32),
            pltpu.VMEM((4, 5, 8, size_z), F32),
            pltpu.VMEM((4, 5, 8, size_z), F32),
            pltpu.VMEM((STEPS - 1, 4) + wide, F32),
            pltpu.VMEM(flow_field.shape, F32),
            pltpu.VMEM((n_cfd, 4, SLOTS), F32),
            pltpu.VMEM((STEPS // 2, n_cfd, 8, SLOTS), F32),
            pltpu.VMEM((size_x * size_y, SLOTS), BF16),
            pltpu.VMEM((3, TARGETS, SLOTS), F32),
            pltpu.VMEM((n_cfd, 4, TARGETS, SLOTS), F32),
            pltpu.VMEM((n_cfd, SAMPLES, SLOTS), BF16),
            pltpu.VMEM((SAMPLES, STEPS * TARGETS), F32),
            pltpu.VMEM((TARGETS, SAMPLES), F32),
            pltpu.VMEM((n_obs - 1, owned, SAMPLES), F32),
            dma((8,)),
            dma((8,)),
            dma((n_z,)),
            dma((n_z,)),
            dma((n_y,)),
            dma((n_y,)),
            dma((STEPS // 2, n_z)),
            dma((STEPS // 2, n_z)),
            dma((STEPS // 2, n_y)),
            dma((STEPS // 2, n_y)),
            dma((n_obs - 1,)),
            dma((n_obs - 1,)),
        ],
        compiler_params=pltpu.CompilerParams(
            collective_id=0, has_side_effects=True, vmem_limit_bytes=64 * 1024 * 1024
        ),
    )(flow_field, disk_mask, surf_cell, delay_bin, tap_phase, panel_counts, observer_pos)


def solution(mesh):
    n_cfd, n_obs = mesh.shape["cfd"], mesh.shape["obs"]
    n_y = 4 if n_cfd >= 16 else 2
    rings = (n_y, n_cfd // n_y, n_obs)
    return jax.shard_map(
        functools.partial(per_device, rings),
        mesh=mesh,
        in_specs=(
            P(None, "cfd", "obs", None),
            P("cfd", "obs", None),
            P("obs", "cfd"),
            P("obs", "cfd"),
            P("obs", "cfd"),
            P(),
            P(None, "cfd"),
        ),
        out_specs=(P(None, "cfd", "obs", None), P(("cfd", "obs"), None)),
        check_vma=False,
    )
```

```python
import functools

import jax
import jax.numpy as jnp
from jax import lax
from jax.experimental import pallas as pl
from jax.experimental.pallas import tpu as pltpu
from jax.sharding import PartitionSpec as P

STEPS = 4
SAMPLES = 512
SLOTS = 128
TARGETS = 128
WIDTH = 4
SIDE = 8
MESH = pl.DeviceIdType.MESH
F32 = jnp.float32
BF16 = jnp.bfloat16


def kernel(
    rings,
    flow_in,
    disk_in,
    cells_in,
    delays_in,
    phases_in,
    counts_in,
    spots_in,
    flow_out,
    signal,
    disk,
    cells,
    delays,
    phases,
    counts,
    spots,
    in_sem,
    wide,
    y_send,
    y_recv,
    corner_send,
    corner_recv,
    state,
    last,
    meta,
    values,
    onehot,
    towards,
    greens,
    bands,
    sums,
    whole,
    parts,
    halo_send,
    halo_recv,
    meta_z_send,
    meta_z_recv,
    meta_y_send,
    meta_y_recv,
    val_z_send,
    val_z_recv,
    val_y_send,
    val_y_recv,
    part_send,
    part_recv,
):
    n_y, n_z, n_obs = rings
    n_cfd = n_y * n_z
    cfd = lax.axis_index("cfd")
    obs = lax.axis_index("obs")
    here_y = cfd // n_z
    here_z = cfd % n_z
    size_x, size_y, size_z = flow_in.shape[1:]
    owned = TARGETS // n_obs
    own_x = slice(WIDTH, WIDTH + size_x)
    own_y = slice(SIDE, SIDE + size_y)
    tall = size_y + 2 * SIDE

    def along_z(far):
        return here_y * n_z + lax.rem(here_z + far, n_z)

    def along_y(far):
        return lax.rem(here_y + far, n_y) * n_z + here_z

    def along_obs(far):
        return lax.rem(obs + far, n_obs)

    cfd_next, cfd_prev = lax.rem(cfd + 1, n_cfd), lax.rem(cfd + n_cfd - 1, n_cfd)
    obs_next, obs_prev = along_obs(1), along_obs(n_obs - 1)

    barrier = pltpu.get_barrier_semaphore()

    def greet(to_cfd, to_obs):
        pl.semaphore_signal(barrier, inc=1, device_id=(to_cfd, to_obs), device_id_type=MESH)

    for far in sorted(range(1, n_z), key=lambda far: abs(far - n_z // 2)):
        greet(along_z(far), obs)
    for to_cfd in (cfd_next, cfd_prev):
        for to_obs in (obs_next, obs_prev, obs):
            greet(to_cfd, to_obs)
    for far in range(1, n_y):
        greet(along_y(far), obs)
    for far in range(1, n_obs):
        greet(cfd, along_obs(far))

    inputs = [
        pltpu.make_async_copy(src, dst, in_sem.at[i])
        for i, (src, dst) in enumerate(
            [
                (disk_in, disk),
                (flow_in, wide.at[0:4, own_x, own_y]),
                (cells_in, cells),
                (delays_in, delays),
                (phases_in, phases),
                (counts_in, counts),
                (spots_in, spots),
            ]
        )
    ]
    for copy in inputs:
        copy.start()

    inputs[0].wait()
    for i in range(size_x):
        wide[4, WIDTH + i, own_y] = disk[i].astype(F32)
    for copy in inputs[1:]:
        copy.wait()

    cell = cells[...]
    row_of = cell >> 7
    live_at = (lax.broadcasted_iota(jnp.int32, counts.shape, 0) == obs) & (
        lax.broadcasted_iota(jnp.int32, counts.shape, 1) == cfd
    )
    own = jnp.sum(jnp.where(live_at, counts[...], 0).astype(F32), axis=(0, 1), keepdims=True)
    live = lax.broadcasted_iota(jnp.int32, (1, SLOTS), 1).astype(F32) < own
    meta[cfd] = jnp.concatenate(
        [
            cell.astype(F32),
            delays[...].astype(F32),
            phases[...].astype(F32),
            jnp.zeros((1, SLOTS), F32),
        ],
        axis=0,
    )

    last_x, last_y = WIDTH + size_x - 1, SIDE + size_y - 1
    corners = [
        (x_side, y_side)
        for x_side in ((cfd_next, last_x, -1, WIDTH - 1), (cfd_prev, WIDTH, 1, last_x + 1))
        for y_side in ((obs_next, True), (obs_prev, False))
    ]

    def pack():
        y_send[0] = wide[:, own_x, last_y - WIDTH + 1 : last_y + 1]
        y_send[1] = wide[:, own_x, SIDE : SIDE + WIDTH]
        for at, ((_, x, turn, _), (_, upper)) in enumerate(corners):
            for c in range(5):
                pieces = []
                for far in range(1, WIDTH):
                    many = WIDTH - far
                    rows = slice(last_y + 1 - many, last_y + 1) if upper else slice(SIDE, SIDE + many)
                    pieces.append(wide[c, x + turn * (far - 1), rows])
                corner_send[at, c] = jnp.concatenate(pieces + [jnp.zeros((2, size_z), F32)], axis=0)

    def unpack_y():
        wide[:, own_x, SIDE - WIDTH : SIDE] = y_recv[0]
        wide[:, own_x, last_y + 1 : last_y + 1 + WIDTH] = y_recv[1]

    def unpack_corners():
        for at, ((_, _, turn, x), (_, upper)) in enumerate(corners):
            for c in range(5):
                begin = 0
                for far in range(1, WIDTH):
                    many = WIDTH - far
                    rows = slice(SIDE - many, SIDE) if upper else slice(last_y + 1, last_y + 1 + many)
                    wide[c, x + turn * (far - 1), rows] = corner_recv[at, c, begin : begin + many]
                    begin += many

    def halo_copies():
        moves = [
            (y_send.at[0], y_recv.at[0], cfd, obs_next),
            (y_send.at[1], y_recv.at[1], cfd, obs_prev),
            (wide.at[:, size_x : size_x + WIDTH, own_y], wide.at[:, 0:WIDTH, own_y], cfd_next, obs),
            (
                wide.at[:, WIDTH : 2 * WIDTH, own_y],
                wide.at[:, WIDTH + size_x : 2 * WIDTH + size_x, own_y],
                cfd_prev,
                obs,
            ),
        ]
        for at, ((to_cfd, _, _, _), (to_obs, _)) in enumerate(corners):
            moves.append((corner_send.at[at], corner_recv.at[at], to_cfd, to_obs))
        return [
            pltpu.make_async_remote_copy(
                src_ref=source,
                dst_ref=target,
                send_sem=halo_send.at[i],
                recv_sem=halo_recv.at[i],
                device_id=(to_cfd, to_obs),
                device_id_type=MESH,
            )
            for i, (source, target, to_cfd, to_obs) in enumerate(moves)
        ]

    def fields(step):
        return wide if step == 0 else state.at[step - 1]

    def outside_x(step):
        ref = fields(step)

        @pl.when(cfd == 0)
        def _():
            ref[0:4, 0:WIDTH] = jnp.zeros((4, WIDTH, tall, size_z), F32)

        @pl.when(cfd == n_cfd - 1)
        def _():
            ref[0:4, WIDTH + size_x :] = jnp.zeros((4, WIDTH, tall, size_z), F32)

    def outside_y(step):
        ref = fields(step)

        @pl.when(obs == 0)
        def _():
            ref[0:4, :, 0:SIDE] = jnp.zeros((4, size_x + 2 * WIDTH, SIDE, size_z), F32)

        @pl.when(obs == n_obs - 1)
        def _():
            ref[0:4, :, SIDE + size_y :] = jnp.zeros((4, size_x + 2 * WIDTH, SIDE, size_z), F32)

    lane = lax.broadcasted_iota(jnp.int32, (tall, size_z), 1)

    def advance(step, begin, end):
        ref = fields(step)
        final = step == STEPS - 1

        @pl.loop(begin, end, unroll=True)
        def _(i):
            slabs = [ref[c, i] for c in range(4)]
            there = wide[4, i]
            for c in range(4):
                q = slabs[c]
                near = (
                    q
                    + ref[c, i + 1]
                    + pltpu.roll(q, 1, 0)
                    + pltpu.roll(q, tall - 1, 0)
                    + jnp.where(lane == 0, 0.0, pltpu.roll(q, 1, 1))
                    + jnp.where(lane == size_z - 1, 0.0, pltpu.roll(q, size_z - 1, 1))
                )
                pull = 0.5 * slabs[1] if c == 0 else -0.4 * q
                moved = 0.1 * near + 0.4 * ref[c, i - 1] + there * pull
                if final:
                    last[c, i - WIDTH] = moved[own_y]
                else:
                    state[step, c, i] = moved

    def sample(step):
        for c in range(4):
            block = last[c] if step == STEPS - 1 else state[step, c, own_x, own_y]
            q = block.reshape(size_x * size_y, size_z)
            high = q.astype(BF16)
            low = (q - high.astype(F32)).astype(BF16)
            dims = (((0,), (0,)), ((), ()))
            lines = lax.dot_general(high, onehot[...], dims, preferred_element_type=F32)
            lines = lines + lax.dot_general(low, onehot[...], dims, preferred_element_type=F32)
            z_at = lax.broadcasted_iota(jnp.int32, (size_z, SLOTS), 0) == (cells[...] & 127)
            v = jnp.sum(jnp.where(z_at, lines, 0.0), axis=0, keepdims=True)
            at = step % 2 * 4 + c
            values[step // 2, cfd, at : at + 1, :] = jnp.where(live, v, 0.0)

    def z_copy(buf, block, send, recv, far, source):
        return pltpu.make_async_remote_copy(
            src_ref=buf.at[block],
            dst_ref=buf.at[block],
            send_sem=send.at[far],
            recv_sem=recv.at[source],
            device_id=(along_z(far), obs),
            device_id_type=MESH,
        )

    def z_start(buf, send, recv):
        @pl.loop(0, n_z - 1, unroll=True)
        def _(k):
            far = n_z // 2 + (1 - 2 * (k % 2)) * ((k + 1) // 2)
            z_copy(buf, cfd, send, recv, far, far).start()

    def z_wait(buf, send, recv):
        @pl.loop(1, n_z, unroll=True)
        def _(far):
            source = here_y * n_z + lax.rem(here_z + n_z - far, n_z)
            z_copy(buf, source, send, recv, far, far).wait_recv()

    def z_wait_send(buf, send, recv):
        @pl.loop(1, n_z, unroll=True)
        def _(far):
            z_copy(buf, cfd, send, recv, far, far).wait_send()

    def y_group(buf, group, send, recv, far):
        block = pl.ds(pl.multiple_of(group * n_z, n_z), n_z)
        return pltpu.make_async_remote_copy(
            src_ref=buf.at[block],
            dst_ref=buf.at[block],
            send_sem=send.at[far],
            recv_sem=recv.at[far],
            device_id=(along_y(far), obs),
            device_id_type=MESH,
        )

    def group_at(back):
        return lax.rem(here_y + n_y - back, n_y)

    def y_start(buf, send, recv):
        for far in range(1, n_y):
            y_group(buf, here_y, send, recv, far).start()

    def y_wait_recv(buf, send, recv, far):
        y_group(buf, group_at(far), send, recv, far).wait_recv()

    def y_wait_send(buf, send, recv):
        for far in range(1, n_y):
            y_group(buf, here_y, send, recv, far).wait_send()

    def prepare(group):
        at = lax.broadcasted_iota(jnp.int32, (16, SLOTS), 0).astype(F32)
        none = jnp.zeros((16, SLOTS), BF16)

        @pl.loop(0, n_z, unroll=4)
        def _(k):
            block = group * n_z + k
            rows = meta[block]
            where = rows[0:1]
            slab = jnp.floor(where * (1.0 / (size_y * size_z)))
            inner = where - float(size_y * size_z) * slab
            line = jnp.floor(inner * (1.0 / size_z))
            place = [
                slab + ((block * size_x).astype(F32) + 0.5),
                line + ((obs * size_y).astype(F32) + 0.5),
                inner - float(size_z) * line + 0.5,
            ]
            delay = rows[1:2]
            frac = rows[2:3] * 0.25
            weights = [
                -frac * (frac - 1.0) * (frac - 2.0) / 6.0,
                (frac + 1.0) * (frac - 1.0) * (frac - 2.0) * 0.5,
                -(frac + 1.0) * frac * (frac - 2.0) * 0.5,
                (frac + 1.0) * frac * (frac - 1.0) / 6.0,
            ]
            high = jnp.floor(delay * 0.0625)
            low = delay - 16.0 * high
            first, second = jnp.zeros((16, SLOTS), F32), jnp.zeros((16, SLOTS), F32)
            for tap in range(4):
                first = jnp.where(at == low + float(tap), weights[tap], first)
                second = jnp.where(at + 16.0 == low + float(tap), weights[tap], second)
            first, second = first.astype(BF16), second.astype(BF16)
            high = jnp.broadcast_to(high, (16, SLOTS)).astype(BF16)
            before = None
            for part in range(SAMPLES // 16):
                here = high == jnp.asarray(float(part), BF16)
                band = jnp.where(here, first, none)
                if before is not None:
                    band = jnp.where(before, second, band)
                bands[block, pl.ds(part * 16, 16), :] = band
                before = here
            for start in range(0, TARGETS, 32):
                part = pl.ds(start, 32)
                d = [towards[a, part, :] - place[a] for a in range(3)]
                inv = lax.rsqrt(d[0] * d[0] + d[1] * d[1] + d[2] * d[2] + 16.0)
                four = 4.0 * inv
                square = four * inv
                greens[block, 0, part, :] = four
                for a in range(3):
                    greens[block, a + 1, part, :] = square * d[a]

    def radiate(group, steps):
        start = group * n_z
        columns = []
        for j in range(n_z):
            block = start + j
            v = [values[step // 2, block, step % 2 * 4 : step % 2 * 4 + 4] for step in steps]
            pieces = [[] for _ in steps]
            for begin in range(0, TARGETS, 32):
                green = [greens[block, c, pl.ds(begin, 32), :] for c in range(4)]
                for at in range(len(steps)):
                    term = green[0] * v[at][0:1]
                    for c in range(1, 4):
                        term = term + green[c] * v[at][c : c + 1]
                    pieces[at].append(term.astype(BF16))
            columns.append(jnp.concatenate([piece for step in pieces for piece in step], axis=0))
        rhs = jnp.concatenate(columns, axis=1)
        lhs = jnp.concatenate([bands[start + j] for j in range(n_z)], axis=1)
        span = slice(steps[0] * TARGETS, (steps[-1] + 1) * TARGETS)
        out = lax.dot_general(lhs, rhs, (((1,), (1,)), ((), ())), preferred_element_type=F32)
        sums[:, span] += out

    def meta_refs():
        return (meta, meta_z_send, meta_z_recv)

    def meta_y_refs():
        return (meta, meta_y_send, meta_y_recv)

    def val_refs(half):
        return (values.at[half], val_z_send.at[half], val_z_recv.at[half])

    def val_y_refs(half):
        return (values.at[half], val_y_send.at[half], val_y_recv.at[half])

    pack()
    pl.semaphore_wait(barrier, 6 + n_z - 1 + n_y - 1 + n_obs - 1)
    result_copy = pltpu.make_async_copy(last, flow_out, in_sem.at[len(inputs)])
    halos = halo_copies()
    for copy in halos[2:] + halos[:2]:
        copy.start()
    z_start(*meta_refs())
    onehot[...] = jnp.where(
        lax.broadcasted_iota(jnp.int32, (size_x * size_y, SLOTS), 0) == row_of, 1.0, 0.0
    ).astype(BF16)
    extent = (size_x * n_cfd, size_y * n_obs, size_z)
    for a in range(3):
        line = spots[a : a + 1] * float(extent[a])
        towards[a] = jnp.transpose(jnp.broadcast_to(line, (SLOTS, TARGETS)))
    for copy in halos[:2]:
        copy.wait()
    unpack_y()
    outside_y(0)
    for step in range(STEPS):
        advance(step, WIDTH + 1 + step, WIDTH + size_x - 1 - step)
        if step < STEPS - 1:
            outside_y(step + 1)
    for copy in halos[2:]:
        copy.wait()
    unpack_corners()
    outside_x(0)
    outside_y(0)
    for step in range(STEPS):
        advance(step, 1 + step, WIDTH + 1 + step)
        advance(step, WIDTH + size_x - 1 - step, 2 * WIDTH + size_x - 1 - step)
        if step < STEPS - 1:
            outside_x(step + 1)
            outside_y(step + 1)
        if step % 2 == 1:
            sample(step - 1)
            sample(step)
            z_start(*val_refs(step // 2))
        if step == 1:
            z_wait(*meta_refs())
            y_start(*meta_y_refs())
    result_copy.start()
    prepare(here_y)

    def arrival(k):
        return 1 + 2 * (k - 1) % (n_y - 1)

    @pl.loop(1, n_y)
    def _(k):
        far = arrival(k)
        y_wait_recv(*meta_y_refs(), far)
        prepare(group_at(far))

    for half in range(2):
        z_wait(*val_refs(half))
        y_start(*val_y_refs(half))
    sums[...] = jnp.zeros_like(sums)
    radiate(here_y, range(STEPS))
    for half in range(2):

        @pl.loop(1, n_y)
        def _(k):
            far = arrival(k)
            y_wait_recv(*val_y_refs(half), far)
            radiate(group_at(far), (2 * half, 2 * half + 1))

    total = sums[:, :TARGETS]
    for step in range(1, STEPS):
        total = total + pltpu.roll(sums[:, step * TARGETS : (step + 1) * TARGETS], step, 0)
    whole[...] = jnp.transpose(total)

    def part_copy(far):
        return pltpu.make_async_remote_copy(
            src_ref=whole.at[pl.ds(pl.multiple_of(along_obs(far) * owned, owned), owned)],
            dst_ref=parts.at[far - 1],
            send_sem=part_send.at[far - 1],
            recv_sem=part_recv.at[far - 1],
            device_id=(cfd, along_obs(far)),
            device_id_type=MESH,
        )

    for far in sorted(range(1, n_obs), key=lambda far: abs(far - n_obs // 2)):
        part_copy(far).start()
    z_wait_send(*meta_refs())
    y_wait_send(*meta_y_refs())
    for half in range(2):
        z_wait_send(*val_refs(half))
        y_wait_send(*val_y_refs(half))
    result_copy.wait()
    result = whole[pl.ds(pl.multiple_of(obs * owned, owned), owned), :]
    for far in range(1, n_obs):
        part_copy(far).wait()
        result = result + parts[far - 1]
    signal[...] = result


def per_device(rings, flow_field, disk_mask, surf_cell, delay_bin, tap_phase, panel_counts, observer_pos):
    n_y, n_z, n_obs = rings
    n_cfd = n_y * n_z
    _, size_x, size_y, size_z = flow_field.shape
    wide = (size_x + 2 * WIDTH, size_y + 2 * SIDE, size_z)
    owned = TARGETS // n_obs
    dma = pltpu.SemaphoreType.DMA
    anywhere = pl.BlockSpec(memory_space=pl.ANY)
    vmem = pl.BlockSpec(memory_space=pltpu.VMEM)
    return pl.pallas_call(
        functools.partial(kernel, rings),
        out_shape=(
            jax.ShapeDtypeStruct(flow_field.shape, F32),
            jax.ShapeDtypeStruct((owned, SAMPLES), F32),
        ),
        in_specs=[anywhere] * 7,
        out_specs=(anywhere, vmem),
        scratch_shapes=[
            pltpu.VMEM(disk_mask.shape, jnp.int32),
            pltpu.VMEM(surf_cell.shape, jnp.int32),
            pltpu.VMEM(delay_bin.shape, jnp.int32),
            pltpu.VMEM(tap_phase.shape, jnp.int32),
            pltpu.VMEM(panel_counts.shape, jnp.int32),
            pltpu.VMEM(observer_pos.shape, F32),
            dma((8,)),
            pltpu.VMEM((5,) + wide, F32),
            pltpu.VMEM((2, 5, size_x, WIDTH, size_z), F32),
            pltpu.VMEM((2, 5, size_x, WIDTH, size_z), F32),
            pltpu.VMEM((4, 5, 8, size_z), F32),
            pltpu.VMEM((4, 5, 8, size_z), F32),
            pltpu.VMEM((STEPS - 1, 4) + wide, F32),
            pltpu.VMEM(flow_field.shape, F32),
            pltpu.VMEM((n_cfd, 4, SLOTS), F32),
            pltpu.VMEM((STEPS // 2, n_cfd, 8, SLOTS), F32),
            pltpu.VMEM((size_x * size_y, SLOTS), BF16),
            pltpu.VMEM((3, TARGETS, SLOTS), F32),
            pltpu.VMEM((n_cfd, 4, TARGETS, SLOTS), F32),
            pltpu.VMEM((n_cfd, SAMPLES, SLOTS), BF16),
            pltpu.VMEM((SAMPLES, STEPS * TARGETS), F32),
            pltpu.VMEM((TARGETS, SAMPLES), F32),
            pltpu.VMEM((n_obs - 1, owned, SAMPLES), F32),
            dma((8,)),
            dma((8,)),
            dma((n_z,)),
            dma((n_z,)),
            dma((n_y,)),
            dma((n_y,)),
            dma((STEPS // 2, n_z)),
            dma((STEPS // 2, n_z)),
            dma((STEPS // 2, n_y)),
            dma((STEPS // 2, n_y)),
            dma((n_obs - 1,)),
            dma((n_obs - 1,)),
        ],
        compiler_params=pltpu.CompilerParams(
            collective_id=0, has_side_effects=True, vmem_limit_bytes=64 * 1024 * 1024
        ),
    )(flow_field, disk_mask, surf_cell, delay_bin, tap_phase, panel_counts, observer_pos)


def solution(mesh):
    n_cfd, n_obs = mesh.shape["cfd"], mesh.shape["obs"]
    n_y = 4 if n_cfd >= 16 else 2
    rings = (n_y, n_cfd // n_y, n_obs)
    return jax.shard_map(
        functools.partial(per_device, rings),
        mesh=mesh,
        in_specs=(
            P(None, "cfd", "obs", None),
            P("cfd", "obs", None),
            P("obs", "cfd"),
            P("obs", "cfd"),
            P("obs", "cfd"),
            P(),
            P(None, "cfd"),
        ),
        out_specs=(P(None, "cfd", "obs", None), P(("cfd", "obs"), None)),
        check_vma=False,
    )
```

```python
import functools

import jax
import jax.numpy as jnp
from jax import lax
from jax.experimental import pallas as pl
from jax.experimental.pallas import tpu as pltpu
from jax.sharding import PartitionSpec as P

STEPS = 4
SAMPLES = 512
SLOTS = 128
TARGETS = 128
WIDTH = 4
SIDE = 8
MESH = pl.DeviceIdType.MESH
F32 = jnp.float32
BF16 = jnp.bfloat16


def kernel(
    rings,
    flow_in,
    disk_in,
    cells_in,
    delays_in,
    phases_in,
    counts_in,
    spots_in,
    flow_out,
    signal,
    disk,
    cells,
    delays,
    phases,
    counts,
    spots,
    in_sem,
    wide,
    y_send,
    y_recv,
    corner_send,
    corner_recv,
    state,
    last,
    meta,
    values,
    onehot,
    towards,
    greens,
    bands,
    sums,
    whole,
    parts,
    halo_send,
    halo_recv,
    meta_z_send,
    meta_z_recv,
    meta_y_send,
    meta_y_recv,
    val_z_send,
    val_z_recv,
    val_y_send,
    val_y_recv,
    part_send,
    part_recv,
):
    n_y, n_z, n_obs = rings
    n_cfd = n_y * n_z
    cfd = lax.axis_index("cfd")
    obs = lax.axis_index("obs")
    here_y = cfd // n_z
    here_z = cfd % n_z
    size_x, size_y, size_z = flow_in.shape[1:]
    owned = TARGETS // n_obs
    own_x = slice(WIDTH, WIDTH + size_x)
    own_y = slice(SIDE, SIDE + size_y)
    tall = size_y + 2 * SIDE

    def along_z(far):
        return here_y * n_z + lax.rem(here_z + far, n_z)

    def along_y(far):
        return lax.rem(here_y + far, n_y) * n_z + here_z

    def along_obs(far):
        return lax.rem(obs + far, n_obs)

    cfd_next, cfd_prev = lax.rem(cfd + 1, n_cfd), lax.rem(cfd + n_cfd - 1, n_cfd)
    obs_next, obs_prev = along_obs(1), along_obs(n_obs - 1)

    barrier = pltpu.get_barrier_semaphore()

    def greet(to_cfd, to_obs):
        pl.semaphore_signal(barrier, inc=1, device_id=(to_cfd, to_obs), device_id_type=MESH)

    for far in sorted(range(1, n_z), key=lambda far: abs(far - n_z // 2)):
        greet(along_z(far), obs)
    for to_cfd in (cfd_next, cfd_prev):
        for to_obs in (obs_next, obs_prev, obs):
            greet(to_cfd, to_obs)
    for far in range(1, n_y):
        greet(along_y(far), obs)
    for far in range(1, n_obs):
        greet(cfd, along_obs(far))

    inputs = [
        pltpu.make_async_copy(src, dst, in_sem.at[i])
        for i, (src, dst) in enumerate(
            [
                (disk_in, disk),
                (flow_in, wide.at[0:4, own_x, own_y]),
                (cells_in, cells),
                (delays_in, delays),
                (phases_in, phases),
                (counts_in, counts),
                (spots_in, spots),
            ]
        )
    ]
    for copy in inputs:
        copy.start()

    inputs[0].wait()
    for i in range(size_x):
        wide[4, WIDTH + i, own_y] = disk[i].astype(F32)
    for copy in inputs[1:]:
        copy.wait()

    cell = cells[...]
    row_of = cell >> 7
    live_at = (lax.broadcasted_iota(jnp.int32, counts.shape, 0) == obs) & (
        lax.broadcasted_iota(jnp.int32, counts.shape, 1) == cfd
    )
    own = jnp.sum(jnp.where(live_at, counts[...], 0).astype(F32), axis=(0, 1), keepdims=True)
    live = lax.broadcasted_iota(jnp.int32, (1, SLOTS), 1).astype(F32) < own
    meta[cfd] = jnp.concatenate(
        [
            cell.astype(F32),
            delays[...].astype(F32),
            phases[...].astype(F32),
            jnp.zeros((1, SLOTS), F32),
        ],
        axis=0,
    )

    last_x, last_y = WIDTH + size_x - 1, SIDE + size_y - 1
    corners = [
        (x_side, y_side)
        for x_side in ((cfd_next, last_x, -1, WIDTH - 1), (cfd_prev, WIDTH, 1, last_x + 1))
        for y_side in ((obs_next, True), (obs_prev, False))
    ]

    def pack():
        y_send[0] = wide[:, own_x, last_y - WIDTH + 1 : last_y + 1]
        y_send[1] = wide[:, own_x, SIDE : SIDE + WIDTH]
        for at, ((_, x, turn, _), (_, upper)) in enumerate(corners):
            for c in range(5):
                pieces = []
                for far in range(1, WIDTH):
                    many = WIDTH - far
                    rows = slice(last_y + 1 - many, last_y + 1) if upper else slice(SIDE, SIDE + many)
                    pieces.append(wide[c, x + turn * (far - 1), rows])
                corner_send[at, c] = jnp.concatenate(pieces + [jnp.zeros((2, size_z), F32)], axis=0)

    def unpack_y():
        wide[:, own_x, SIDE - WIDTH : SIDE] = y_recv[0]
        wide[:, own_x, last_y + 1 : last_y + 1 + WIDTH] = y_recv[1]

    def unpack_corners():
        for at, ((_, _, turn, x), (_, upper)) in enumerate(corners):
            for c in range(5):
                begin = 0
                for far in range(1, WIDTH):
                    many = WIDTH - far
                    rows = slice(SIDE - many, SIDE) if upper else slice(last_y + 1, last_y + 1 + many)
                    wide[c, x + turn * (far - 1), rows] = corner_recv[at, c, begin : begin + many]
                    begin += many

    def halo_copies():
        moves = [
            (y_send.at[0], y_recv.at[0], cfd, obs_next),
            (y_send.at[1], y_recv.at[1], cfd, obs_prev),
            (wide.at[:, size_x : size_x + WIDTH, own_y], wide.at[:, 0:WIDTH, own_y], cfd_next, obs),
            (
                wide.at[:, WIDTH : 2 * WIDTH, own_y],
                wide.at[:, WIDTH + size_x : 2 * WIDTH + size_x, own_y],
                cfd_prev,
                obs,
            ),
        ]
        for at, ((to_cfd, _, _, _), (to_obs, _)) in enumerate(corners):
            moves.append((corner_send.at[at], corner_recv.at[at], to_cfd, to_obs))
        return [
            pltpu.make_async_remote_copy(
                src_ref=source,
                dst_ref=target,
                send_sem=halo_send.at[i],
                recv_sem=halo_recv.at[i],
                device_id=(to_cfd, to_obs),
                device_id_type=MESH,
            )
            for i, (source, target, to_cfd, to_obs) in enumerate(moves)
        ]

    def fields(step):
        return wide if step == 0 else state.at[step - 1]

    def outside_x(step):
        ref = fields(step)

        @pl.when(cfd == 0)
        def _():
            ref[0:4, 0:WIDTH] = jnp.zeros((4, WIDTH, tall, size_z), F32)

        @pl.when(cfd == n_cfd - 1)
        def _():
            ref[0:4, WIDTH + size_x :] = jnp.zeros((4, WIDTH, tall, size_z), F32)

    def outside_y(step):
        ref = fields(step)

        @pl.when(obs == 0)
        def _():
            ref[0:4, :, 0:SIDE] = jnp.zeros((4, size_x + 2 * WIDTH, SIDE, size_z), F32)

        @pl.when(obs == n_obs - 1)
        def _():
            ref[0:4, :, SIDE + size_y :] = jnp.zeros((4, size_x + 2 * WIDTH, SIDE, size_z), F32)

    lane = lax.broadcasted_iota(jnp.int32, (tall, size_z), 1)

    def advance(step, begin, end):
        ref = fields(step)
        final = step == STEPS - 1

        @pl.loop(begin, end, unroll=True)
        def _(i):
            slabs = [ref[c, i] for c in range(4)]
            there = wide[4, i]
            for c in range(4):
                q = slabs[c]
                near = (
                    q
                    + ref[c, i + 1]
                    + pltpu.roll(q, 1, 0)
                    + pltpu.roll(q, tall - 1, 0)
                    + jnp.where(lane == 0, 0.0, pltpu.roll(q, 1, 1))
                    + jnp.where(lane == size_z - 1, 0.0, pltpu.roll(q, size_z - 1, 1))
                )
                pull = 0.5 * slabs[1] if c == 0 else -0.4 * q
                moved = 0.1 * near + 0.4 * ref[c, i - 1] + there * pull
                if final:
                    last[c, i - WIDTH] = moved[own_y]
                else:
                    state[step, c, i] = moved

    def sample(step):
        for c in range(4):
            block = last[c] if step == STEPS - 1 else state[step, c, own_x, own_y]
            q = block.reshape(size_x * size_y, size_z)
            high = q.astype(BF16)
            low = (q - high.astype(F32)).astype(BF16)
            dims = (((0,), (0,)), ((), ()))
            lines = lax.dot_general(high, onehot[...], dims, preferred_element_type=F32)
            lines = lines + lax.dot_general(low, onehot[...], dims, preferred_element_type=F32)
            z_at = lax.broadcasted_iota(jnp.int32, (size_z, SLOTS), 0) == (cells[...] & 127)
            v = jnp.sum(jnp.where(z_at, lines, 0.0), axis=0, keepdims=True)
            at = step % 2 * 4 + c
            values[step // 2, cfd, at : at + 1, :] = jnp.where(live, v, 0.0)

    def z_copy(buf, block, send, recv, far, source):
        return pltpu.make_async_remote_copy(
            src_ref=buf.at[block],
            dst_ref=buf.at[block],
            send_sem=send.at[far],
            recv_sem=recv.at[source],
            device_id=(along_z(far), obs),
            device_id_type=MESH,
        )

    def z_start(buf, send, recv):
        @pl.loop(0, n_z - 1, unroll=True)
        def _(k):
            far = n_z // 2 + (1 - 2 * (k % 2)) * ((k + 1) // 2)
            z_copy(buf, cfd, send, recv, far, far).start()

    def z_wait(buf, send, recv):
        @pl.loop(1, n_z, unroll=True)
        def _(far):
            source = here_y * n_z + lax.rem(here_z + n_z - far, n_z)
            z_copy(buf, source, send, recv, far, far).wait_recv()

    def z_wait_send(buf, send, recv):
        @pl.loop(1, n_z, unroll=True)
        def _(far):
            z_copy(buf, cfd, send, recv, far, far).wait_send()

    def y_group(buf, group, send, recv, far):
        block = pl.ds(pl.multiple_of(group * n_z, n_z), n_z)
        return pltpu.make_async_remote_copy(
            src_ref=buf.at[block],
            dst_ref=buf.at[block],
            send_sem=send.at[far],
            recv_sem=recv.at[far],
            device_id=(along_y(far), obs),
            device_id_type=MESH,
        )

    def group_at(back):
        return lax.rem(here_y + n_y - back, n_y)

    def y_start(buf, send, recv):
        for far in range(1, n_y):
            y_group(buf, here_y, send, recv, far).start()

    def y_wait_recv(buf, send, recv, far):
        y_group(buf, group_at(far), send, recv, far).wait_recv()

    def y_wait_send(buf, send, recv):
        for far in range(1, n_y):
            y_group(buf, here_y, send, recv, far).wait_send()

    def prepare(group):
        at = lax.broadcasted_iota(jnp.int32, (16, SLOTS), 0).astype(F32)
        none = jnp.zeros((16, SLOTS), BF16)

        @pl.loop(0, n_z, unroll=4)
        def _(k):
            block = group * n_z + k
            rows = meta[block]
            where = rows[0:1]
            slab = jnp.floor(where * (1.0 / (size_y * size_z)))
            inner = where - float(size_y * size_z) * slab
            line = jnp.floor(inner * (1.0 / size_z))
            place = [
                slab + ((block * size_x).astype(F32) + 0.5),
                line + ((obs * size_y).astype(F32) + 0.5),
                inner - float(size_z) * line + 0.5,
            ]
            delay = rows[1:2]
            frac = rows[2:3] * 0.25
            weights = [
                -frac * (frac - 1.0) * (frac - 2.0) / 6.0,
                (frac + 1.0) * (frac - 1.0) * (frac - 2.0) * 0.5,
                -(frac + 1.0) * frac * (frac - 2.0) * 0.5,
                (frac + 1.0) * frac * (frac - 1.0) / 6.0,
            ]
            high = jnp.floor(delay * 0.0625)
            low = delay - 16.0 * high
            first, second = jnp.zeros((16, SLOTS), F32), jnp.zeros((16, SLOTS), F32)
            for tap in range(4):
                first = jnp.where(at == low + float(tap), weights[tap], first)
                second = jnp.where(at + 16.0 == low + float(tap), weights[tap], second)
            first, second = first.astype(BF16), second.astype(BF16)
            high = jnp.broadcast_to(high, (16, SLOTS)).astype(BF16)
            before = None
            for part in range(SAMPLES // 16):
                here = high == jnp.asarray(float(part), BF16)
                band = jnp.where(here, first, none)
                if before is not None:
                    band = jnp.where(before, second, band)
                bands[block, pl.ds(part * 16, 16), :] = band
                before = here
            for start in range(0, TARGETS, 32):
                part = pl.ds(start, 32)
                d = [towards[a, part, :] - place[a] for a in range(3)]
                inv = lax.rsqrt(d[0] * d[0] + d[1] * d[1] + d[2] * d[2] + 16.0)
                four = 4.0 * inv
                square = four * inv
                greens[block, 0, part, :] = four.astype(BF16).astype(F32)
                for a in range(3):
                    greens[block, a + 1, part, :] = (square * d[a]).astype(BF16).astype(F32)

    def radiate(group, steps):
        start = group * n_z
        columns = []
        for j in range(n_z):
            block = start + j
            v = [values[step // 2, block, step % 2 * 4 : step % 2 * 4 + 4] for step in steps]
            pieces = [[] for _ in steps]
            for begin in range(0, TARGETS, 32):
                green = [greens[block, c, pl.ds(begin, 32), :] for c in range(4)]
                for at in range(len(steps)):
                    term = green[0] * v[at][0:1]
                    for c in range(1, 4):
                        term = term + green[c] * v[at][c : c + 1]
                    pieces[at].append(term.astype(BF16))
            columns.append(jnp.concatenate([piece for step in pieces for piece in step], axis=0))
        rhs = jnp.concatenate(columns, axis=1)
        lhs = jnp.concatenate([bands[start + j] for j in range(n_z)], axis=1)
        span = slice(steps[0] * TARGETS, (steps[-1] + 1) * TARGETS)
        out = lax.dot_general(lhs, rhs, (((1,), (1,)), ((), ())), preferred_element_type=F32)
        sums[:, span] += out

    def meta_refs():
        return (meta, meta_z_send, meta_z_recv)

    def meta_y_refs():
        return (meta, meta_y_send, meta_y_recv)

    def val_refs(half):
        return (values.at[half], val_z_send.at[half], val_z_recv.at[half])

    def val_y_refs(half):
        return (values.at[half], val_y_send.at[half], val_y_recv.at[half])

    pack()
    pl.semaphore_wait(barrier, 6 + n_z - 1 + n_y - 1 + n_obs - 1)
    result_copy = pltpu.make_async_copy(last, flow_out, in_sem.at[len(inputs)])
    halos = halo_copies()
    for copy in halos[2:] + halos[:2]:
        copy.start()
    z_start(*meta_refs())
    onehot[...] = jnp.where(
        lax.broadcasted_iota(jnp.int32, (size_x * size_y, SLOTS), 0) == row_of, 1.0, 0.0
    ).astype(BF16)
    extent = (size_x * n_cfd, size_y * n_obs, size_z)
    for a in range(3):
        line = spots[a : a + 1] * float(extent[a])
        towards[a] = jnp.transpose(jnp.broadcast_to(line, (SLOTS, TARGETS)))
    for copy in halos[:2]:
        copy.wait()
    unpack_y()
    outside_y(0)
    for step in range(STEPS):
        advance(step, WIDTH + 1 + step, WIDTH + size_x - 1 - step)
        if step < STEPS - 1:
            outside_y(step + 1)
    for copy in halos[2:]:
        copy.wait()
    unpack_corners()
    outside_x(0)
    outside_y(0)
    for step in range(STEPS):
        advance(step, 1 + step, WIDTH + 1 + step)
        advance(step, WIDTH + size_x - 1 - step, 2 * WIDTH + size_x - 1 - step)
        if step < STEPS - 1:
            outside_x(step + 1)
            outside_y(step + 1)
        if step % 2 == 1:
            sample(step - 1)
            sample(step)
            z_start(*val_refs(step // 2))
        if step == 1:
            z_wait(*meta_refs())
            y_start(*meta_y_refs())
    result_copy.start()
    prepare(here_y)

    def arrival(k):
        return 1 + 2 * (k - 1) % (n_y - 1)

    @pl.loop(1, n_y)
    def _(k):
        far = arrival(k)
        y_wait_recv(*meta_y_refs(), far)
        prepare(group_at(far))

    for half in range(2):
        z_wait(*val_refs(half))
        y_start(*val_y_refs(half))
    sums[...] = jnp.zeros_like(sums)
    radiate(here_y, range(STEPS))
    for half in range(2):

        @pl.loop(1, n_y)
        def _(k):
            far = arrival(k)
            y_wait_recv(*val_y_refs(half), far)
            radiate(group_at(far), (2 * half, 2 * half + 1))

    total = sums[:, :TARGETS]
    for step in range(1, STEPS):
        total = total + pltpu.roll(sums[:, step * TARGETS : (step + 1) * TARGETS], step, 0)
    whole[...] = jnp.transpose(total)

    def part_copy(far):
        return pltpu.make_async_remote_copy(
            src_ref=whole.at[pl.ds(pl.multiple_of(along_obs(far) * owned, owned), owned)],
            dst_ref=parts.at[far - 1],
            send_sem=part_send.at[far - 1],
            recv_sem=part_recv.at[far - 1],
            device_id=(cfd, along_obs(far)),
            device_id_type=MESH,
        )

    for far in sorted(range(1, n_obs), key=lambda far: abs(far - n_obs // 2)):
        part_copy(far).start()
    z_wait_send(*meta_refs())
    y_wait_send(*meta_y_refs())
    for half in range(2):
        z_wait_send(*val_refs(half))
        y_wait_send(*val_y_refs(half))
    result_copy.wait()
    result = whole[pl.ds(pl.multiple_of(obs * owned, owned), owned), :]
    for far in range(1, n_obs):
        part_copy(far).wait()
        result = result + parts[far - 1]
    signal[...] = result


def per_device(rings, flow_field, disk_mask, surf_cell, delay_bin, tap_phase, panel_counts, observer_pos):
    n_y, n_z, n_obs = rings
    n_cfd = n_y * n_z
    _, size_x, size_y, size_z = flow_field.shape
    wide = (size_x + 2 * WIDTH, size_y + 2 * SIDE, size_z)
    owned = TARGETS // n_obs
    dma = pltpu.SemaphoreType.DMA
    anywhere = pl.BlockSpec(memory_space=pl.ANY)
    vmem = pl.BlockSpec(memory_space=pltpu.VMEM)
    return pl.pallas_call(
        functools.partial(kernel, rings),
        out_shape=(
            jax.ShapeDtypeStruct(flow_field.shape, F32),
            jax.ShapeDtypeStruct((owned, SAMPLES), F32),
        ),
        in_specs=[anywhere] * 7,
        out_specs=(anywhere, vmem),
        scratch_shapes=[
            pltpu.VMEM(disk_mask.shape, jnp.int32),
            pltpu.VMEM(surf_cell.shape, jnp.int32),
            pltpu.VMEM(delay_bin.shape, jnp.int32),
            pltpu.VMEM(tap_phase.shape, jnp.int32),
            pltpu.VMEM(panel_counts.shape, jnp.int32),
            pltpu.VMEM(observer_pos.shape, F32),
            dma((8,)),
            pltpu.VMEM((5,) + wide, F32),
            pltpu.VMEM((2, 5, size_x, WIDTH, size_z), F32),
            pltpu.VMEM((2, 5, size_x, WIDTH, size_z), F32),
            pltpu.VMEM((4, 5, 8, size_z), F32),
            pltpu.VMEM((4, 5, 8, size_z), F32),
            pltpu.VMEM((STEPS - 1, 4) + wide, F32),
            pltpu.VMEM(flow_field.shape, F32),
            pltpu.VMEM((n_cfd, 4, SLOTS), F32),
            pltpu.VMEM((STEPS // 2, n_cfd, 8, SLOTS), F32),
            pltpu.VMEM((size_x * size_y, SLOTS), BF16),
            pltpu.VMEM((3, TARGETS, SLOTS), F32),
            pltpu.VMEM((n_cfd, 4, TARGETS, SLOTS), F32),
            pltpu.VMEM((n_cfd, SAMPLES, SLOTS), BF16),
            pltpu.VMEM((SAMPLES, STEPS * TARGETS), F32),
            pltpu.VMEM((TARGETS, SAMPLES), F32),
            pltpu.VMEM((n_obs - 1, owned, SAMPLES), F32),
            dma((8,)),
            dma((8,)),
            dma((n_z,)),
            dma((n_z,)),
            dma((n_y,)),
            dma((n_y,)),
            dma((STEPS // 2, n_z)),
            dma((STEPS // 2, n_z)),
            dma((STEPS // 2, n_y)),
            dma((STEPS // 2, n_y)),
            dma((n_obs - 1,)),
            dma((n_obs - 1,)),
        ],
        compiler_params=pltpu.CompilerParams(
            collective_id=0, has_side_effects=True, vmem_limit_bytes=64 * 1024 * 1024
        ),
    )(flow_field, disk_mask, surf_cell, delay_bin, tap_phase, panel_counts, observer_pos)


def solution(mesh):
    n_cfd, n_obs = mesh.shape["cfd"], mesh.shape["obs"]
    n_y = 4 if n_cfd >= 16 else 2
    rings = (n_y, n_cfd // n_y, n_obs)
    return jax.shard_map(
        functools.partial(per_device, rings),
        mesh=mesh,
        in_specs=(
            P(None, "cfd", "obs", None),
            P("cfd", "obs", None),
            P("obs", "cfd"),
            P("obs", "cfd"),
            P("obs", "cfd"),
            P(),
            P(None, "cfd"),
        ),
        out_specs=(P(None, "cfd", "obs", None), P(("cfd", "obs"), None)),
        check_vma=False,
    )
```
